128 devices in a mesh: lat: 16 (over y, x_hi, core), lon: 8 (over z, x_lo).
Axes of the slice: x: 4 (x_hi: 2, x_lo: 2; x = x_hi * 2 + x_lo), y: 4, z: 4, core: 2. Of those that a mesh axis runs over, the one named last changes fastest.
Arguments:
- fields: bfloat16 [192, 192, 512], P('lat', 'lon'), may hold values from -6 to 6
- region_fine: int32 [192, 192], P('lat', 'lon'), may hold values from 0 to 3
- region_coarse: int32 [96, 96], P('lat', 'lon'), may hold values from 0 to 3
- gain_fine: float32 [512], replicated, may hold values from 0.5 to 1.5
- qkv_fine: bfloat16 [512, 1536], replicated, may hold values from -0.25 to 0.25
- bias_fine: bfloat16 [8, 72, 72], replicated, may hold values from -4 to 360, as said below
- out_fine: bfloat16 [512, 512], replicated, may hold values from -0.25 to 0.25
- gain_merge: float32 [2048], replicated, may hold values from 0.5 to 1.5
- merge_weight: bfloat16 [2048, 1024], replicated, may hold values from -0.125 to 0.125
- gain_coarse: float32 [1024], replicated, may hold values from 0.5 to 1.5
- qkv_coarse: bfloat16 [1024, 3072], P(None, 'lat'), may hold values from -0.1875 to 0.1875
- bias_coarse: bfloat16 [16, 72, 72], P('lat'), may hold values from -4 to 360, as said below
- out_coarse: bfloat16 [1024, 1024], P('lat'), may hold values from -0.1875 to 0.1875
- grad_skip: bfloat16 [192, 192, 512], P('lat', 'lon'), may hold values from -6 to 6
- grad_out: bfloat16 [96, 96, 1024], P('lat', 'lon'), may hold values from -6 to 6
Outputs:
- skip_level: bfloat16 [192, 192, 512], P('lat', 'lon')
- output: bfloat16 [96, 96, 1024], P('lat', 'lon')
- grad_fields: bfloat16 [192, 192, 512], P('lat', 'lon')
- grad_gain_fine: float32 [512], replicated
- grad_qkv_fine: float32 [512, 1536], replicated
- grad_bias_fine: float32 [8, 72, 72], replicated
- grad_out_fine: float32 [512, 512], replicated
- grad_gain_merge: float32 [2048], replicated
- grad_merge_weight: float32 [2048, 1024], P(None, ('lat', 'lon'))
- grad_gain_coarse: float32 [1024], replicated
- grad_qkv_coarse: float32 [1024, 3072], P(None, 'lat')
- grad_bias_coarse: float32 [16, 72, 72], P('lat')
- grad_out_coarse: float32 [1024, 1024], P('lat')
The draws below stay inside these ranges and needn't reach their ends.
Inputs may be any that keep to these rules, and one draw needn't show every extreme that they name: `bias_fine`: relative position bias entries; in some draws a few entries of some rows are large and positive. `bias_coarse`: relative position bias entries; in some draws a few entries of some rows are large and positive.
All inputs are finite; a program needn't handle non-finite values.
Results may differ from the reference program's by a relative error of at most 0.03.
Values may be sent and summed in bfloat16 or wider, within the bound.
No kernel may reach another device: no remote copies, remote signals or barrier semaphores. Data moves between devices by JAX's collectives and lax.ppermute only.
A program may use at most 128 MiB of HBM per device.

```python
import jax
import jax.numpy as jnp
from jax import lax

D = 512
D2 = 1024
H1 = 8
H2 = 16
WLAT = 6
WLON = 12
SLAT = 3
SLON = 6
NLAT = 192
NLON = 192
NLAT2 = 96
NLON2 = 96


def drawn_table(key, head_count):
    cells = WLAT * WLON
    return 1.5 * jax.random.truncated_normal(key, -2.5, 2.5, (head_count, cells, cells), jnp.float32)


def draw_bias_fine(key, part):
    key = jax.random.fold_in(key, 11)
    return drawn_table(key, H1).astype(jnp.bfloat16)


def draw_bias_coarse(key, part):
    key = jax.random.fold_in(key, 13)
    return drawn_table(key, H2).astype(jnp.bfloat16)


def with_ends(entries, own_key, smallest, high):
    index_at = [jax.random.randint(jax.random.fold_in(own_key, axis), (), 0, length) for axis, length in enumerate(entries.shape)]
    main_axis = entries.shape.index(max(entries.shape))
    next_to = index_at[:main_axis] + [(index_at[main_axis] + 1) % entries.shape[main_axis]] + index_at[main_axis + 1:]
    return entries.at[tuple(index_at)].set(smallest).at[tuple(next_to)].set(high)


def steps_of(stream_key, shape, pieces, low, top_value):
    loudness, own = 1.0, jax.random.fold_in(stream_key, 6)
    for dim, blocks in pieces:
        heights = jnp.exp(jax.random.uniform(jax.random.fold_in(own, dim), (blocks,), jnp.float32, low / len(pieces), top_value / len(pieces)))
        loudness = loudness * jnp.repeat(heights, shape[dim] // blocks).reshape([-1 if axis == dim else 1 for axis in range(len(shape))])
    return loudness


def gaussian(stream_key, dims, width, reach, split=(), dtype=jnp.bfloat16):
    array = width * jax.random.normal(stream_key, dims, jnp.float32)
    if split:
        array = array * steps_of(stream_key, dims, split, -0.22, 0.18)
    return jnp.clip(array, -reach, reach).astype(dtype)


def setup_inputs(seed: int = 0) -> dict:
    keys = jax.random.split(jax.random.key(seed), 16)
    return {
        "fields": gaussian(keys[0], (NLAT, NLON, D), 1.0, 6.0, ((0, 16), (1, 8))),
        "region_fine": with_ends(jax.random.randint(keys[1], (NLAT, NLON), 0, 4), jax.random.fold_in(keys[1], 1), 0, 3).astype(jnp.int32),
        "region_coarse": with_ends(jax.random.randint(keys[2], (NLAT2, NLON2), 0, 4), jax.random.fold_in(keys[2], 1), 0, 3).astype(jnp.int32),
        "gain_fine": jnp.clip(1.0 + 0.1 * jax.random.normal(keys[3], (D,), jnp.float32), 0.5, 1.5),
        "qkv_fine": gaussian(keys[4], (D, 3 * D), D ** -0.5, 0.25),
        "bias_fine": draw_bias_fine(jax.random.fold_in(keys[15], 71), 0),
        "out_fine": gaussian(keys[6], (D, D), D ** -0.5, 0.25),
        "gain_merge": jnp.clip(1.0 + 0.1 * jax.random.normal(keys[7], (4 * D,), jnp.float32), 0.5, 1.5),
        "merge_weight": gaussian(keys[8], (4 * D, D2), (4 * D) ** -0.5, 0.125),
        "gain_coarse": jnp.clip(1.0 + 0.1 * jax.random.normal(keys[9], (D2,), jnp.float32), 0.5, 1.5),
        "qkv_coarse": gaussian(keys[10], (D2, 3 * D2), D2 ** -0.5, 0.1875, ((1, 16),)),
        "bias_coarse": draw_bias_coarse(jax.random.fold_in(keys[15], 71), 0),
        "out_coarse": gaussian(keys[12], (D2, D2), D2 ** -0.5, 0.1875, ((0, 16),)),
        "grad_skip": gaussian(keys[13], (NLAT, NLON, D), 1.0, 6.0, ((0, 16), (1, 8))),
        "grad_out": gaussian(keys[14], (NLAT2, NLON2, D2), 1.0, 6.0, ((0, 16), (1, 8))),
    }


EPSILON = 1e-05
MASKED = -1000000000.0
HIGHEST = lax.Precision.HIGHEST

def layer_norm(values, gain_row):
    average = lax.optimization_barrier(jnp.mean(values, -1, keepdims=True))
    centred = values - average
    spread = lax.optimization_barrier(jnp.mean(centred * centred, -1, keepdims=True))
    return centred * lax.rsqrt(spread + EPSILON) * gain_row

def windows(grid_cells):
    rows_all, cols_all, channels = grid_cells.shape
    reshaped = grid_cells.reshape(rows_all // WLAT, WLAT, cols_all // WLON, WLON, channels)
    return reshaped.transpose(0, 2, 1, 3, 4).reshape(-1, WLAT * WLON, channels)

def unwindows(blocks, rows_all, cols_all):
    channels = blocks.shape[-1]
    reshaped = blocks.reshape(rows_all // WLAT, cols_all // WLON, WLAT, WLON, channels)
    return reshaped.transpose(0, 2, 1, 3, 4).reshape(rows_all, cols_all, channels)

def window_masks(region):
    labels = windows(region[:, :, None])[:, :, 0]
    return labels[:, :, None] == labels[:, None, :]

def attention_core(queries, key_rows, value_rows, bias_table, allowed):
    factor = queries.shape[-1] ** (-0.5)
    scores = jnp.einsum('nqhd,nkhd->nhqk', queries.astype(jnp.float32), key_rows.astype(jnp.float32), precision=HIGHEST) * factor
    scores = jnp.where(allowed[:, None], scores + bias_table.astype(jnp.float32)[None], MASKED)
    row_top = lax.optimization_barrier(jnp.max(scores, -1, keepdims=True))
    weights = jnp.exp(scores - row_top)
    probability = weights / lax.optimization_barrier(jnp.sum(weights, -1, keepdims=True))
    rounded = probability.astype(jnp.bfloat16)
    context = jnp.einsum('nhqk,nkhd->nqhd', rounded.astype(jnp.float32), value_rows.astype(jnp.float32), precision=HIGHEST)
    return (probability, rounded, context)

def attention_back(grad_context, queries, key_rows, value_rows, probability, rounded):
    factor = queries.shape[-1] ** (-0.5)
    grad_prob = jnp.einsum('nqhd,nkhd->nhqk', grad_context.astype(jnp.float32), value_rows.astype(jnp.float32), precision=HIGHEST)
    grad_prob = lax.optimization_barrier(grad_prob.astype(jnp.bfloat16)).astype(jnp.float32)
    grad_value = jnp.einsum('nhqk,nqhd->nkhd', rounded.astype(jnp.float32), grad_context.astype(jnp.float32), precision=HIGHEST)
    inner = lax.optimization_barrier(jnp.sum(grad_prob * probability, -1, keepdims=True))
    grad_scores = probability * (grad_prob - inner)
    grad_bias = lax.optimization_barrier(jnp.sum(grad_scores, 0))
    scores_low = grad_scores.astype(jnp.bfloat16).astype(jnp.float32)
    grad_query = jnp.einsum('nhqk,nkhd->nqhd', scores_low, key_rows.astype(jnp.float32), precision=HIGHEST) * factor
    grad_key = jnp.einsum('nhqk,nqhd->nkhd', scores_low, queries.astype(jnp.float32), precision=HIGHEST) * factor
    return (grad_query, grad_key, grad_value, grad_bias)

def attend_forward(window_rows, w_qkv, bias_table, allowed, w_out, head_count):
    window_count, length, features = window_rows.shape
    head_dim = w_qkv.shape[1] // (3 * head_count)
    projected = jnp.dot(window_rows.reshape(window_count * length, features), w_qkv, preferred_element_type=jnp.float32)
    projected = projected.astype(jnp.bfloat16).reshape(window_count, length, head_count, 3, head_dim)
    queries = projected[:, :, :, 0]
    key_rows = projected[:, :, :, 1]
    value_rows = projected[:, :, :, 2]
    probability, rounded, context = attention_core(queries, key_rows, value_rows, bias_table, allowed)
    context = context.astype(jnp.bfloat16).reshape(window_count * length, head_count * head_dim)
    result = jnp.dot(context, w_out, preferred_element_type=jnp.float32)
    return (result.reshape(window_count, length, w_out.shape[1]), (queries, key_rows, value_rows, probability, rounded, context))

def attend_backward(window_rows, w_qkv, w_out, saved, grad_rows, head_count):
    window_count, length, features = window_rows.shape
    head_dim = w_qkv.shape[1] // (3 * head_count)
    queries, key_rows, value_rows, probability, rounded, context = saved
    grad_flat = grad_rows.reshape(window_count * length, grad_rows.shape[2])
    grad_out_w = jnp.dot(context.T, grad_flat, preferred_element_type=jnp.float32)
    grad_context = jnp.dot(grad_flat, w_out.T, preferred_element_type=jnp.float32).astype(jnp.bfloat16)
    grad_context = grad_context.reshape(window_count, length, head_count, head_dim)
    grad_query, grad_key, grad_value, grad_bias = attention_back(grad_context, queries, key_rows, value_rows, probability, rounded)
    grad_proj = jnp.stack([grad_query, grad_key, grad_value], 3).astype(jnp.bfloat16)
    grad_proj = grad_proj.reshape(window_count * length, 3 * head_count * head_dim)
    flat_rows = window_rows.reshape(window_count * length, features)
    grad_qkv_w = jnp.dot(flat_rows.T, grad_proj, preferred_element_type=jnp.float32)
    grad_input = jnp.dot(grad_proj, w_qkv.T, preferred_element_type=jnp.float32).reshape(window_count, length, features)
    return (grad_input, grad_qkv_w, grad_bias, grad_out_w)

def to_patches(grid_cells):
    rows_all, cols_all, channels = grid_cells.shape
    reshaped = grid_cells.reshape(rows_all // 2, 2, cols_all // 2, 2, channels)
    return reshaped.transpose(0, 2, 1, 3, 4).reshape(rows_all // 2, cols_all // 2, 4 * channels)

def from_patches(patches):
    rows_half, cols_half, wide = patches.shape
    reshaped = patches.reshape(rows_half, cols_half, 2, 2, wide // 4)
    return reshaped.transpose(0, 2, 1, 3, 4).reshape(2 * rows_half, 2 * cols_half, wide // 4)

def roll_grid(grid_cells):
    return jnp.roll(grid_cells, (-SLAT, -SLON), (0, 1))

def unroll_grid(grid_cells):
    return jnp.roll(grid_cells, (SLAT, SLON), (0, 1))

def reference(fields, region_fine, region_coarse, gain_fine, qkv_fine, bias_fine, out_fine, gain_merge, merge_weight, gain_coarse, qkv_coarse, bias_coarse, out_coarse, grad_skip, grad_out):
    rows_fine, cols_fine = (fields.shape[0], fields.shape[1])
    rolled = roll_grid(fields).astype(jnp.float32)
    normed, fine_pull = jax.vjp(layer_norm, rolled, gain_fine)
    fine_rows = windows(normed.astype(jnp.bfloat16))
    fine_mask = window_masks(region_fine)
    fine_part, fine_saved = attend_forward(fine_rows, qkv_fine, bias_fine, fine_mask, out_fine, H1)
    skip_level = unroll_grid((rolled + unwindows(fine_part, rows_fine, cols_fine)).astype(jnp.bfloat16))
    patches = to_patches(skip_level).astype(jnp.float32)
    merged, merge_pull = jax.vjp(layer_norm, patches, gain_merge)
    merged = merged.astype(jnp.bfloat16)
    rows_coarse, cols_coarse, width_in = merged.shape
    merged_flat = merged.reshape(-1, width_in)
    coarse = jnp.dot(merged_flat, merge_weight, preferred_element_type=jnp.float32).astype(jnp.bfloat16)
    coarse = coarse.reshape(rows_coarse, cols_coarse, -1)
    coarse32 = coarse.astype(jnp.float32)
    coarse_normed, coarse_pull = jax.vjp(layer_norm, coarse32, gain_coarse)
    coarse_rows = windows(roll_grid(coarse_normed.astype(jnp.bfloat16)))
    coarse_mask = window_masks(region_coarse)
    head_total, coarse_saved = attend_forward(coarse_rows, qkv_coarse, bias_coarse, coarse_mask, out_coarse, H2)
    output = (coarse32 + unroll_grid(unwindows(head_total, rows_coarse, cols_coarse))).astype(jnp.bfloat16)
    grad_rows = windows(roll_grid(grad_out))
    grad_windows, grad_qkv_c, grad_bias_c, grad_out_c = attend_backward(coarse_rows, qkv_coarse, out_coarse, coarse_saved, grad_rows, H2)
    grad_normed = unroll_grid(unwindows(grad_windows, rows_coarse, cols_coarse)).astype(jnp.bfloat16)
    grad_coarse_ln, grad_gain_c = coarse_pull(grad_normed.astype(jnp.float32))
    grad_coarse = (grad_out.astype(jnp.float32) + grad_coarse_ln).astype(jnp.bfloat16).reshape(-1, D2)
    grad_merged = jnp.dot(grad_coarse, merge_weight.T, preferred_element_type=jnp.float32)
    grad_merge_w = jnp.dot(merged_flat.T, grad_coarse, preferred_element_type=jnp.float32)
    grad_patches, grad_gain_m = merge_pull(grad_merged.reshape(rows_coarse, cols_coarse, width_in))
    grad_skip_all = (grad_skip.astype(jnp.float32) + from_patches(grad_patches)).astype(jnp.bfloat16)
    grad_rolled = roll_grid(grad_skip_all)
    grad_fine, grad_qkv_f, grad_bias_f, grad_out_f = attend_backward(fine_rows, qkv_fine, out_fine, fine_saved, windows(grad_rolled), H1)
    grad_fine_ln, grad_gain_f = fine_pull(unwindows(grad_fine, rows_fine, cols_fine))
    grad_fields = unroll_grid((grad_rolled.astype(jnp.float32) + grad_fine_ln).astype(jnp.bfloat16))
    return (skip_level, output, grad_fields, grad_gain_f, grad_qkv_f, grad_bias_f, grad_out_f, grad_gain_m, grad_merge_w, grad_gain_c, grad_qkv_c, grad_bias_c, grad_out_c)
```

```python
import jax
import jax.numpy as jnp
import numpy as np
from jax import lax
from jax.experimental import pallas as pl
from jax.experimental.pallas import tpu as pltpu
from jax.sharding import Mesh
from jax.sharding import PartitionSpec as P

EPSILON = 1e-05
MASKED = -1000000000.0
BF = jnp.bfloat16
F32 = jnp.float32
CELLS = 72
PAD = 80
SCALE = 0.125

LAT = ("y", "xh", "c")
LON = ("z", "xl")
ALL = LAT + LON
CHIPS = ("y", "xh", "z", "xl")
PARTS = 640


def fine_window_row(rr, cc):
    return (rr // 6 * 2 + cc // 12) * PAD + (rr % 6) * 12 + cc % 12


def make_fine_roll():
    m = np.zeros((320, 496), np.float32)
    for rr in range(12):
        for cc in range(24):
            if rr < 9 and cc < 18:
                s = (rr + 3) * 24 + cc + 6
            elif cc < 18:
                s = 288 + (rr - 9) * 24 + cc + 6
            elif rr < 9:
                s = 368 + (rr + 3) * 8 + cc - 18
            else:
                s = 464 + (rr - 9) * 8 + cc - 18
            m[fine_window_row(rr, cc), s] = 1
    return m


def make_fine_send():
    m = np.zeros((160, 320), np.float32)
    for r in range(3):
        for cc in range(18):
            m[r * 18 + cc, fine_window_row(9 + r, cc)] = 1
    for rr in range(9):
        for q in range(6):
            m[64 + rr * 6 + q, fine_window_row(rr, 18 + q)] = 1
    for r in range(3):
        for q in range(6):
            m[128 + r * 6 + q, fine_window_row(9 + r, 18 + q)] = 1
    return m


def make_fine_unroll():
    m = np.zeros((288, 480), np.float32)
    for r in range(12):
        for c in range(24):
            if r >= 3 and c >= 6:
                s = fine_window_row(r - 3, c - 6)
            elif c >= 6:
                s = 320 + r * 18 + c - 6
            elif r >= 3:
                s = 384 + (r - 3) * 6 + c
            else:
                s = 448 + r * 6 + c
            m[r * 24 + c, s] = 1
    return m


def patch_order():
    order = []
    for ro in range(2):
        for co in range(2):
            for r in range(6):
                for c in range(12):
                    order.append((2 * r + ro) * 24 + 2 * c + co)
    return np.array(order)


def make_fine_halo():
    m = np.zeros((128, 288), np.float32)
    for r in range(12):
        for c in range(8):
            m[r * 8 + c, r * 24 + c] = 1
    for r in range(4):
        for c in range(8):
            m[96 + r * 8 + c, r * 24 + c] = 1
    return m


def make_coarse_send():
    m = np.zeros((96, 72), np.float32)
    for r in range(3):
        for c in range(6):
            m[r * 6 + c, r * 12 + c + 6] = 1
            m[32 + r * 6 + c, (r + 3) * 12 + c] = 1
            m[64 + r * 6 + c, r * 12 + c] = 1
    return m


def make_coarse_roll():
    own = np.zeros((PAD, 72), np.float32)
    far = np.zeros((PAD, 96), np.float32)
    for a in range(6):
        for b in range(12):
            row = a * 12 + b
            if a < 3 and b < 6:
                own[row, (a + 3) * 12 + b + 6] = 1
            elif b < 6:
                far[row, (a - 3) * 6 + b] = 1
            elif a < 3:
                far[row, 32 + a * 6 + b - 6] = 1
            else:
                far[row, 64 + (a - 3) * 6 + b - 6] = 1
    return own, far


def make_coarse_back():
    m = np.zeros((96, PAD), np.float32)
    for r in range(3):
        for c in range(6):
            m[r * 6 + c, (r + 3) * 12 + c] = 1
            m[32 + r * 6 + c, r * 12 + c + 6] = 1
            m[64 + r * 6 + c, (r + 3) * 12 + c + 6] = 1
    return m


def make_coarse_unroll():
    own = np.zeros((72, PAD), np.float32)
    far = np.zeros((72, 96), np.float32)
    for r in range(6):
        for c in range(12):
            row = r * 12 + c
            if r >= 3 and c >= 6:
                own[row, (r - 3) * 12 + c - 6] = 1
            elif c >= 6:
                far[row, r * 6 + c - 6] = 1
            elif r >= 3:
                far[row, 32 + (r - 3) * 6 + c] = 1
            else:
                far[row, 64 + r * 6 + c] = 1
    return own, far


def const(m):
    return jnp.asarray(np.asarray(m, np.float32), BF)


def nn(a, b):
    return lax.dot_general(a, b, (((1,), (0,)), ((), ())), preferred_element_type=F32)


def nt(a, b):
    return lax.dot_general(a, b, (((1,), (1,)), ((), ())), preferred_element_type=F32)


def tn(a, b):
    return lax.dot_general(a, b, (((0,), (0,)), ((), ())), preferred_element_type=F32)


def normalise(x):
    average = jnp.mean(x, -1, keepdims=True)
    centred = x - average
    rstd = lax.rsqrt(jnp.mean(centred * centred, -1, keepdims=True) + EPSILON)
    return centred * rstd, rstd


def norm_back(dy, gain, xhat, rstd):
    dxhat = dy * gain
    m1 = jnp.mean(dxhat, -1, keepdims=True)
    m2 = jnp.mean(dxhat * xhat, -1, keepdims=True)
    return rstd * (dxhat - m1 - xhat * m2)


def allowed_cells(label_row):
    across = jnp.broadcast_to(label_row, (PAD, PAD))
    return across.T == across


def probabilities(q, k, bias_t, allowed):
    scores = nt(k, q) * SCALE + bias_t
    scores = jnp.where(allowed, scores, MASKED)
    weights = jnp.exp(scores - jnp.max(scores, 0, keepdims=True))
    return weights * (1.0 / jnp.sum(weights, 0, keepdims=True))


def score_grad(p, v, dc):
    dp = nt(v, dc)
    inner = jnp.sum(dp * p, 0, keepdims=True)
    return p * (dp - inner)


def call(body, outs, *args, scratch=(), flops=4_000_000_000):
    shapes = [jax.ShapeDtypeStruct(s, d) for s, d in outs]
    return pl.pallas_call(
        body,
        out_shape=shapes,
        scratch_shapes=list(scratch),
        compiler_params=pltpu.CompilerParams(vmem_limit_bytes=40 * 1024 * 1024),
        cost_estimate=pl.CostEstimate(flops=flops, bytes_accessed=4_000_000, transcendentals=0),
    )(*args)


def fine_forward(
    f, hl, hn, hd, roll, gain, wqkv, wo, bias, lab, send,
    xr_o, xn_o, qkv_o, p_o, c_o, skip_o, b_o, l_o, d_o,
):
    src = jnp.concatenate([f[...], hl[...], hn[...], hd[...]], 0)
    xr = nn(roll[...], src)
    xr_o[...] = xr.astype(BF)
    xhat, _ = normalise(xr)
    xn = (xhat * gain[...]).astype(BF)
    xn_o[...] = xn
    qkv_o[...] = nn(xn, wqkv[...]).astype(BF)
    for w in range(4):
        allowed = allowed_cells(lab[w : w + 1, :])
        rows = slice(w * PAD, (w + 1) * PAD)
        for h in range(8):
            at = 192 * h
            q = qkv_o[rows, at : at + 64]
            k = qkv_o[rows, at + 64 : at + 128]
            v = qkv_o[rows, at + 128 : at + 192]
            p = probabilities(q, k, bias[h].astype(F32), allowed).astype(BF)
            p_o[w * 8 + h] = p
            c_o[rows, 64 * h : 64 * h + 64] = tn(p, v).astype(BF)
    skip = (xr + nn(c_o[...], wo[...])).astype(BF)
    skip_o[...] = skip
    pieces = nn(send[...], skip).astype(BF)
    b_o[...] = pieces[:64]
    l_o[...] = pieces[64:128]
    d_o[...] = pieces[128:]


def merge_forward(
    win, b, l, d, unroll, order, gain_m, wm, gain_c, send,
    skip_o, pat_o, mn_o, z_o, zn_o, b_o, l_o, d_o,
):
    src = jnp.concatenate([win[...], b[...], l[...], d[...]], 0)
    skip_o[...] = nn(unroll[...], src).astype(BF)
    cells = nn(order[...], src)
    patches = jnp.concatenate([cells[72 * k : 72 * k + 72] for k in range(4)], 1)
    pat_o[...] = patches.astype(BF)
    mhat, _ = normalise(patches)
    mn = (mhat * gain_m[...]).astype(BF)
    mn_o[0:72, :] = mn
    mn_o[72:80, :] = jnp.zeros((8, 2048), BF)
    z = nn(mn, wm[...]).astype(BF)
    z_o[...] = z
    zhat, _ = normalise(z.astype(F32))
    zn = (zhat * gain_c[...]).astype(BF)
    zn_o[...] = zn
    pieces = nn(send[...], zn).astype(BF)
    b_o[...] = pieces[0:32]
    l_o[...] = pieces[32:64]
    d_o[...] = pieces[64:96]


def coarse_pieces(tile, send, b_o, l_o, d_o):
    pieces = nn(send[...], tile[...]).astype(BF)
    b_o[...] = pieces[0:32]
    l_o[...] = pieces[32:64]
    d_o[...] = pieces[64:96]


def coarse_window(tile, b, l, d, own, far, out):
    src = jnp.concatenate([b[...], l[...], d[...]], 0)
    out[...] = (nn(own[...], tile[...]) + nn(far[...], src)).astype(BF)


def coarse_window_labelled(tile, b, l, d, own, far, lab, out):
    src = jnp.concatenate([b[...], l[...], d[...]], 0)
    rows = nn(own[...], tile[...]) + nn(far[...], src)
    at = lax.broadcasted_iota(jnp.int32, rows.shape, 0)
    out[...] = jnp.where(at == CELLS, jnp.broadcast_to(lab[...], rows.shape), rows).astype(BF)


def coarse_attention(
    u0, u1, u2, u3, g0, g1, g2, g3, w0, w1, w2, w3,
    sd0, sd1, sd2, sd3, gw0, gw1, gw2, gw3,
    qkv, ctx, dqkv, bias_sum,
):
    ws = (w0, w1, w2, w3)
    u = jnp.concatenate([r[...] for r in (u0, u1, u2, u3)], 0)
    live = lax.broadcasted_iota(jnp.int32, (PAD, 1024), 0) < CELLS
    labels = []
    parts = []
    for r in (g0, g1, g2, g3):
        rows = r[...].astype(F32)
        labels.append(rows[CELLS : CELLS + 1, 0:PAD])
        parts.append(jnp.where(live, rows, 0.0).astype(BF))
    g = jnp.concatenate(parts, 0)
    wo = jnp.concatenate([r[192:256, :] for r in ws], 0)
    dc = nt(g, wo).astype(BF)
    for s in range(4):
        qkv[s] = nt(u, ws[s][0:192, :]).astype(BF)
    masks = [allowed_cells(row) for row in labels]
    for s in range(4):
        bias = ws[s][256:336, 0:PAD].astype(F32)
        total = jnp.zeros((PAD, PAD), F32)
        for w in range(4):
            rows = slice(w * PAD, (w + 1) * PAD)
            q = qkv[s, rows, 0:64]
            k = qkv[s, rows, 64:128]
            v = qkv[s, rows, 128:192]
            p = probabilities(q, k, bias, masks[w])
            pb = p.astype(BF)
            ctx[rows, 64 * s : 64 * s + 64] = tn(pb, v).astype(BF)
            dch = dc[rows, 64 * s : 64 * s + 64]
            ds = score_grad(p, v, dch)
            total = total + ds
            dsb = ds.astype(BF)
            dqkv[s, rows, 0:64] = (tn(dsb, k) * SCALE).astype(BF)
            dqkv[s, rows, 64:128] = (nn(dsb, q) * SCALE).astype(BF)
            dqkv[s, rows, 128:192] = nn(pb, dch).astype(BF)
        bias_sum[s] = jnp.zeros((PAD, 1024), F32)
        bias_sum[s, :, 0:PAD] = total
    c = ctx[...]
    out = nn(c, wo)
    du = nn(dqkv[0], w0[0:192, :])
    for s in range(1, 4):
        du = du + nn(dqkv[s], ws[s][0:192, :])
    for w, o in enumerate((sd0, sd1, sd2, sd3)):
        o[0:PAD, :] = out[w * PAD : (w + 1) * PAD].astype(BF)
        o[PAD : 2 * PAD, :] = du[w * PAD : (w + 1) * PAD].astype(BF)
    gwo = tn(c, g).astype(BF)
    for s, o in enumerate((gw0, gw1, gw2, gw3)):
        o[0:192, :] = tn(dqkv[s], u).astype(BF)
        o[192:256, :] = gwo[64 * s : 64 * s + 64]
        o[256:336, :] = bias_sum[s].astype(BF)


def coarse_sum(a0, a1, a2, a3, back, own_o, b_o, l_o, d_o):
    total = a0[...].astype(F32) + a1[...].astype(F32) + a2[...].astype(F32) + a3[...].astype(F32)
    total = total.astype(BF)
    own_o[...] = total
    s = nn(back[...], total[0:PAD]).astype(BF)
    du = nn(back[...], total[PAD:]).astype(BF)
    for i, o in enumerate((b_o, l_o, d_o)):
        o[0:32, :] = s[32 * i : 32 * i + 32]
        o[32:64, :] = du[32 * i : 32 * i + 32]


def merge_backward(
    z, go, own, b, l, d, uown, ufar, gain_c, pat, gain_m, wm, gskip, spread, halo,
    out_o, dskip_o, top_o, side_o, corner_o, dzt_o, gg_m, gg_c,
):
    far_s = jnp.concatenate([b[0:32, :], l[0:32, :], d[0:32, :]], 0)
    far_d = jnp.concatenate([b[32:64, :], l[32:64, :], d[32:64, :]], 0)
    mix = own[...]
    s = nn(uown[...], mix[0:PAD]) + nn(ufar[...], far_s)
    dzn = nn(uown[...], mix[PAD:]) + nn(ufar[...], far_d)
    z32 = z[...].astype(F32)
    out_o[...] = (z32 + s).astype(BF)
    zhat, rstd = normalise(z32)
    gg_c[...] = jnp.sum(dzn * zhat, 0, keepdims=True)
    dz32 = go[...].astype(F32) + norm_back(dzn, gain_c[...], zhat, rstd)
    dz = dz32.astype(BF)
    dzt_o[...] = jnp.zeros((1024, 128), BF)
    dzt_o[:, 0:CELLS] = dz32.T.astype(BF)
    dmn = nt(dz, wm[...])
    mhat, mrstd = normalise(pat[...].astype(F32))
    gg_m[...] = jnp.sum(dmn * mhat, 0, keepdims=True)
    dpat = norm_back(dmn, gain_m[...], mhat, mrstd).astype(BF)
    cells = jnp.concatenate([dpat[:, 512 * k : 512 * k + 512] for k in range(4)], 0)
    dskip = (gskip[...].astype(F32) + nn(spread[...], cells)).astype(BF)
    dskip_o[...] = dskip
    top_o[...] = dskip[0:80]
    extra = nn(halo[...], dskip).astype(BF)
    side_o[...] = extra[0:96]
    corner_o[...] = extra[96:128]


def fine_backward(
    f, hl, hn, hd, roll, gain, wqkv, wo, xr, xn, qkv, p_in, c, send, gg_m, gg_c,
    dx_o, b_o, l_o, d_o, pack_o,
    dqkv, bias_sum,
):
    src = jnp.concatenate([f[...], hl[...], hn[...], hd[...]], 0)
    g32 = nn(roll[...], src)
    g = g32.astype(BF)
    dc = nt(g, wo[...]).astype(BF)
    bias_sum[...] = jnp.zeros((8, PAD, 128), F32)
    for h in range(8):
        at = 192 * h
        total = jnp.zeros((PAD, PAD), F32)
        for w in range(4):
            rows = slice(w * PAD, (w + 1) * PAD)
            q = qkv[rows, at : at + 64]
            k = qkv[rows, at + 64 : at + 128]
            v = qkv[rows, at + 128 : at + 192]
            pb = p_in[w * 8 + h]
            dch = dc[rows, 64 * h : 64 * h + 64]
            ds = score_grad(pb.astype(F32), v, dch)
            total = total + ds
            dsb = ds.astype(BF)
            dqkv[rows, at : at + 64] = (tn(dsb, k) * SCALE).astype(BF)
            dqkv[rows, at + 64 : at + 128] = (nn(dsb, q) * SCALE).astype(BF)
            dqkv[rows, at + 128 : at + 192] = nn(pb, dch).astype(BF)
        bias_sum[h, :, 0:PAD] = total
    dproj = dqkv[...]
    du = nt(dproj, wqkv[...])
    xhat, rstd = normalise(xr[...].astype(F32))
    gg_f = jnp.sum(du * xhat, 0, keepdims=True)
    dx = (g32 + norm_back(du, gain[...], xhat, rstd)).astype(BF)
    dx_o[...] = dx
    pieces = nn(send[...], dx).astype(BF)
    b_o[...] = pieces[:64]
    l_o[...] = pieces[64:128]
    d_o[...] = pieces[128:]
    gq = tn(xn[...], dproj)
    for i in range(12):
        pack_o[32 * i : 32 * i + 32] = gq[:, 128 * i : 128 * i + 128].reshape(32, 16, 128).astype(BF)
    go = tn(c[...], g)
    for i in range(4):
        pack_o[384 + 32 * i : 416 + 32 * i] = (
            go[:, 128 * i : 128 * i + 128].reshape(32, 16, 128).astype(BF)
        )
    for h in range(8):
        pack_o[512 + 5 * h : 517 + 5 * h] = bias_sum[h].reshape(5, 16, 128).astype(BF)
    rows = [gg_f[:, 128 * i : 128 * i + 128] for i in range(4)]
    rows += [gg_m[:, 128 * i : 128 * i + 128] for i in range(16)]
    rows += [gg_c[:, 128 * i : 128 * i + 128] for i in range(8)]
    rows.append(jnp.zeros((4, 128), F32))
    pack_o[552:554] = jnp.concatenate(rows, 0).reshape(2, 16, 128).astype(BF)
    pack_o[554:PARTS] = jnp.zeros((PARTS - 554, 16, 128), BF)


def fine_place(win, b, l, d, unroll, out):
    src = jnp.concatenate([win[...], b[...], l[...], d[...]], 0)
    out[...] = nn(unroll[...], src).astype(BF)


def merge_weight_share(dzt, mn, out):
    total = nn(dzt[0:64, 0:PAD], mn[0:PAD, :])
    for i in range(1, 16):
        total = total + nn(dzt[64 * i : 64 * i + 64, 0:PAD], mn[PAD * i : PAD * i + PAD, :])
    out[...] = total.astype(BF)


def unpack(pack, gq_o, gb_o, go_o, gain_o):
    for i in range(12):
        gq_o[:, 128 * i : 128 * i + 128] = (
            pack[32 * i : 32 * i + 32].astype(F32).reshape(512, 128)
        )
    for i in range(4):
        go_o[:, 128 * i : 128 * i + 128] = (
            pack[384 + 32 * i : 416 + 32 * i].astype(F32).reshape(512, 128)
        )
    for h in range(8):
        t = pack[512 + 5 * h : 517 + 5 * h].astype(F32).reshape(80, 128)
        gb_o[h] = t[:, 0:PAD].T[0:CELLS, 0:CELLS]
    gain_o[...] = pack[552:554].astype(F32).reshape(32, 128)


def count_of(axes):
    n = 1
    for a in axes:
        n *= lax.axis_size(a)
    return n


def shift(x, axes, by):
    n = count_of(axes)
    return lax.ppermute(x, axes, [(i, (i + by) % n) for i in range(n)])


def shift_both(x, by):
    nl, nn_ = count_of(LAT), count_of(LON)
    pairs = [
        (i * nn_ + j, ((i + by) % nl) * nn_ + (j + by) % nn_)
        for i in range(nl)
        for j in range(nn_)
    ]
    return lax.ppermute(x, ALL, pairs)


def exchange(pieces, by):
    lat_piece, lon_piece, corner = pieces
    return shift(lat_piece, LAT, by), shift(lon_piece, LON, by), shift_both(corner, by)


def along_y(x):
    return [x] + [shift(x, ("y",), -k) for k in (1, 2, 3)]


def local(
    fields,
    region_fine,
    region_coarse,
    gain_fine,
    qkv_fine,
    bias_fine,
    out_fine,
    gain_merge,
    merge_weight,
    gain_coarse,
    qkv_coarse,
    bias_coarse,
    out_coarse,
    grad_skip,
    grad_out,
):
    c_roll, c_send, c_unroll = make_fine_roll(), make_fine_send(), make_fine_unroll()
    roll_own, roll_far = make_coarse_roll()
    back_own, back_far = make_coarse_unroll()
    roll_f, send_f, unroll_f = const(c_roll), const(c_send), const(c_unroll)
    order_f = const(c_unroll[patch_order()])
    spread = np.zeros((288, 288), np.float32)
    spread[patch_order(), np.arange(288)] = 1
    spread_f, halo_f = const(spread), const(make_fine_halo())
    send_c, back_c = const(make_coarse_send()), const(make_coarse_back())
    roll_own, roll_far = const(roll_own), const(roll_far)
    back_own, back_far = const(back_own), const(back_far)
    gain_f2, gain_m2, gain_c2 = gain_fine[None], gain_merge[None], gain_coarse[None]

    tile = fields.reshape(288, 512)
    sides = (tile[:80], fields[:, :8].reshape(96, 512), fields[:4, :8].reshape(32, 512))
    f_lat, f_lon, f_corner = exchange(sides, -1)

    bias_t = jnp.pad(jnp.swapaxes(bias_coarse, 1, 2)[0], ((0, 8), (0, 1024 - CELLS)))
    shared = jnp.concatenate([qkv_coarse.T, out_coarse, bias_t], 0)

    go_tile = grad_out.reshape(72, 1024)
    piece = ((32, 1024), BF)
    go_pieces = call(coarse_pieces, [piece] * 3, go_tile, send_c)
    go_far = exchange(go_pieces, -1)
    label_c = jnp.pad(
        region_coarse.reshape(1, 72).astype(F32), ((0, 0), (0, 952)), constant_values=-1.0
    )
    w0 = shared
    w2 = shift(shared, ("xh",), 1)
    w1 = shift(w0, ("c",), 1)
    w3 = shift(w2, ("c",), 1)

    label_f = region_fine.reshape(2, 6, 2, 12).transpose(0, 2, 1, 3).reshape(4, 72).astype(F32)
    label_f = jnp.pad(label_f, ((0, 0), (0, 8)), constant_values=-1.0)
    bias_ft = jnp.pad(jnp.swapaxes(bias_fine, 1, 2), ((0, 0), (0, 8), (0, 8)))

    win = ((320, 512), BF)
    xr, xn, qkv, prob, ctx, skip_win, s_lat, s_lon, s_corner = call(
        fine_forward,
        [win, win, ((320, 1536), BF), ((32, PAD, PAD), BF), win, win,
         ((64, 512), BF), ((64, 512), BF), ((32, 512), BF)],
        tile, f_lat, f_lon, f_corner, roll_f, gain_f2, qkv_fine, out_fine, bias_ft, label_f, send_f,
        flops=10_000_000_000,
    )
    s_far = exchange((s_lat, s_lon, s_corner), 1)
    (gw_win,) = call(
        coarse_window_labelled, [((PAD, 1024), BF)],
        go_tile, *go_far, roll_own, roll_far, label_c,
    )
    g_all = along_y(gw_win)
    skip_level, pat, mn, z, zn, *z_pieces = call(
        merge_forward,
        [((288, 512), BF), ((72, 2048), BF), ((PAD, 2048), BF), ((72, 1024), BF), ((72, 1024), BF),
         piece, piece, piece],
        skip_win, *s_far, unroll_f, order_f, gain_m2, merge_weight, gain_c2, send_c,
    )
    z_far = exchange(z_pieces, -1)
    mn_column = lax.all_gather(mn, LAT, axis=0, tiled=True)
    (u_win,) = call(coarse_window, [((PAD, 1024), BF)], zn, *z_far, roll_own, roll_far)
    u_all = along_y(u_win)
    sd0, sd1, sd2, sd3, gw0, gw1, gw2, gw3 = call(
        coarse_attention,
        [((2 * PAD, 1024), BF)] * 4 + [((336, 1024), BF)] * 4,
        *u_all, *g_all, w0, w1, w2, w3,
        scratch=[
            pltpu.VMEM((4, 320, 192), BF), pltpu.VMEM((320, 256), BF),
            pltpu.VMEM((4, 320, 192), BF), pltpu.VMEM((4, PAD, 1024), F32),
        ],
        flops=10_000_000_000,
    )
    sd = [sd0] + [shift(x, ("y",), k) for k, x in ((1, sd1), (2, sd2), (3, sd3))]
    mix, *mix_pieces = call(
        coarse_sum, [((2 * PAD, 1024), BF)] + [((64, 1024), BF)] * 3, *sd, back_c
    )
    mix_far = exchange(mix_pieces, 1)

    r0 = shift(gw1, ("c",), 1)
    r2 = shift(gw3, ("c",), 1)
    half2 = (gw2.astype(F32) + r2.astype(F32)).astype(BF)
    from_xh = shift(half2, ("xh",), 1)
    mine = (gw0.astype(F32) + r0.astype(F32) + from_xh.astype(F32)).astype(BF)

    output, dskip, k_lat, k_lon, k_corner, dzt, gg_m, gg_c = call(
        merge_backward,
        [((72, 1024), BF), ((288, 512), BF), ((80, 512), BF), ((96, 512), BF), ((32, 512), BF),
         ((1024, 128), BF), ((1, 2048), F32), ((1, 1024), F32)],
        z, go_tile, mix, *mix_far, back_own, back_far, gain_c2, pat, gain_m2, merge_weight,
        grad_skip.reshape(288, 512), spread_f, halo_f,
    )
    k_far = exchange((k_lat, k_lon, k_corner), -1)
    coarse_grads = lax.psum(mine, LON)
    dzt_mine = lax.all_to_all(dzt, LAT, 0, 0, tiled=True)
    dx_win, d_lat, d_lon, d_corner, pack = call(
        fine_backward,
        [win, ((64, 512), BF), ((64, 512), BF), ((32, 512), BF), ((PARTS, 16, 128), BF)],
        dskip, *k_far, roll_f, gain_f2, qkv_fine, out_fine, xr, xn, qkv, prob, ctx, send_f,
        gg_m, gg_c,
        scratch=[pltpu.VMEM((320, 1536), BF), pltpu.VMEM((8, PAD, 128), F32)],
        flops=15_000_000_000,
    )
    d_far = exchange((d_lat, d_lon, d_corner), 1)

    halves = lax.all_to_all(pack.reshape(2, PARTS // 2, 16, 128), "c", 0, 0, tiled=True)
    half = (halves[0].astype(F32) + halves[1].astype(F32)).astype(BF)
    spread_out = lax.all_to_all(half, CHIPS, 0, 0, tiled=True)
    chips = count_of(CHIPS)
    share = PARTS // 2 // chips
    part = jnp.sum(spread_out.reshape(chips, share, 16, 128).astype(F32), 0).astype(BF)
    copies = jnp.broadcast_to(part[None], (chips, share, 16, 128)).reshape(PARTS // 2, 16, 128)
    whole_half = lax.all_to_all(copies, CHIPS, 0, 0, tiled=True)
    whole = lax.all_gather(whole_half, "c", axis=0, tiled=True)

    (merge_t,) = call(merge_weight_share, [((64, 2048), BF)], dzt_mine, mn_column)
    merge_parts = lax.all_to_all(merge_t, LON, 0, 0, tiled=True)
    merge_share = jnp.sum(merge_parts.reshape(8, 8, 2048).astype(F32), 0).T

    (grad_fields,) = call(
        fine_place, [((288, 512), BF)], dx_win, *d_far, unroll_f, flops=200_000_000
    )
    gq, gb, go, gains = call(
        unpack,
        [((512, 1536), F32), ((8, CELLS, CELLS), F32), ((512, 512), F32), ((32, 128), F32)],
        whole,
    )
    return (
        skip_level.reshape(12, 24, 512),
        output.reshape(6, 12, 1024),
        grad_fields.reshape(12, 24, 512),
        gains[0:4].reshape(512),
        gq,
        gb,
        go,
        gains[4:20].reshape(2048),
        merge_share,
        gains[20:28].reshape(1024),
        coarse_grads[0:192].T.astype(F32),
        coarse_grads[256:328, 0:CELLS].T.astype(F32)[None],
        coarse_grads[192:256].astype(F32),
    )


def solution(mesh):
    fine_mesh = Mesh(mesh.devices.reshape(4, 2, 2, 4, 2), ALL)
    grid = P(LAT, LON, None)
    placed = (
        grid,
        P(LAT, LON),
        P(LAT, LON),
        P(),
        P(),
        P(),
        P(),
        P(),
        P(),
        P(),
        P(None, LAT),
        P(LAT, None, None),
        P(LAT, None),
        grid,
        grid,
    )
    return jax.shard_map(
        local,
        mesh=fine_mesh,
        in_specs=placed,
        out_specs=(
            grid,
            grid,
            grid,
            P(),
            P(),
            P(),
            P(),
            P(),
            P(None, ALL),
            P(),
            P(None, LAT),
            P(LAT, None, None),
            P(LAT, None),
        ),
        check_vma=False,
    )
```

```python
import jax
import jax.numpy as jnp
import numpy as np
from jax import lax
from jax.experimental import pallas as pl
from jax.experimental.pallas import tpu as pltpu
from jax.sharding import Mesh
from jax.sharding import PartitionSpec as P

EPSILON = 1e-05
MASKED = -1000000000.0
BF = jnp.bfloat16
F32 = jnp.float32
CELLS = 72
PAD = 80
SCALE = 0.125

LAT = ("y", "xh", "c")
LON = ("z", "xl")
ALL = LAT + LON
CHIPS = ("y", "xh", "z", "xl")
HALF = 320
PARTS = 640


def fine_window_row(rr, cc):
    return (rr // 6 * 2 + cc // 12) * PAD + (rr % 6) * 12 + cc % 12


def make_fine_roll():
    m = np.zeros((320, 496), np.float32)
    for rr in range(12):
        for cc in range(24):
            if rr < 9 and cc < 18:
                s = (rr + 3) * 24 + cc + 6
            elif cc < 18:
                s = 288 + (rr - 9) * 24 + cc + 6
            elif rr < 9:
                s = 368 + (rr + 3) * 8 + cc - 18
            else:
                s = 464 + (rr - 9) * 8 + cc - 18
            m[fine_window_row(rr, cc), s] = 1
    return m


def make_fine_send():
    m = np.zeros((160, 320), np.float32)
    for r in range(3):
        for cc in range(18):
            m[r * 18 + cc, fine_window_row(9 + r, cc)] = 1
    for rr in range(9):
        for q in range(6):
            m[64 + rr * 6 + q, fine_window_row(rr, 18 + q)] = 1
    for r in range(3):
        for q in range(6):
            m[128 + r * 6 + q, fine_window_row(9 + r, 18 + q)] = 1
    return m


def make_fine_unroll():
    m = np.zeros((288, 480), np.float32)
    for r in range(12):
        for c in range(24):
            if r >= 3 and c >= 6:
                s = fine_window_row(r - 3, c - 6)
            elif c >= 6:
                s = 320 + r * 18 + c - 6
            elif r >= 3:
                s = 384 + (r - 3) * 6 + c
            else:
                s = 448 + r * 6 + c
            m[r * 24 + c, s] = 1
    return m


def patch_order():
    order = []
    for ro in range(2):
        for co in range(2):
            for r in range(6):
                for c in range(12):
                    order.append((2 * r + ro) * 24 + 2 * c + co)
    return np.array(order)


def make_coarse_send():
    m = np.zeros((96, 72), np.float32)
    for r in range(3):
        for c in range(6):
            m[r * 6 + c, r * 12 + c + 6] = 1
            m[32 + r * 6 + c, (r + 3) * 12 + c] = 1
            m[64 + r * 6 + c, r * 12 + c] = 1
    return m


def make_coarse_roll():
    own = np.zeros((PAD, 72), np.float32)
    far = np.zeros((PAD, 96), np.float32)
    for a in range(6):
        for b in range(12):
            row = a * 12 + b
            if a < 3 and b < 6:
                own[row, (a + 3) * 12 + b + 6] = 1
            elif b < 6:
                far[row, (a - 3) * 6 + b] = 1
            elif a < 3:
                far[row, 32 + a * 6 + b - 6] = 1
            else:
                far[row, 64 + (a - 3) * 6 + b - 6] = 1
    return own, far


def make_coarse_back():
    m = np.zeros((96, PAD), np.float32)
    for r in range(3):
        for c in range(6):
            m[r * 6 + c, (r + 3) * 12 + c] = 1
            m[32 + r * 6 + c, r * 12 + c + 6] = 1
            m[64 + r * 6 + c, (r + 3) * 12 + c + 6] = 1
    return m


def make_coarse_unroll():
    own = np.zeros((72, PAD), np.float32)
    far = np.zeros((72, 96), np.float32)
    for r in range(6):
        for c in range(12):
            row = r * 12 + c
            if r >= 3 and c >= 6:
                own[row, (r - 3) * 12 + c - 6] = 1
            elif c >= 6:
                far[row, r * 6 + c - 6] = 1
            elif r >= 3:
                far[row, 32 + (r - 3) * 6 + c] = 1
            else:
                far[row, 64 + r * 6 + c] = 1
    return own, far


def const(m):
    return jnp.asarray(np.asarray(m, np.float32), BF)


def nn(a, b):
    return lax.dot_general(a, b, (((1,), (0,)), ((), ())), preferred_element_type=F32)


def nt(a, b):
    return lax.dot_general(a, b, (((1,), (1,)), ((), ())), preferred_element_type=F32)


def tn(a, b):
    return lax.dot_general(a, b, (((0,), (0,)), ((), ())), preferred_element_type=F32)


def normalise(x):
    average = jnp.mean(x, -1, keepdims=True)
    centred = x - average
    rstd = lax.rsqrt(jnp.mean(centred * centred, -1, keepdims=True) + EPSILON)
    return centred * rstd, rstd


def norm_back(dy, gain, xhat, rstd):
    dxhat = dy * gain
    m1 = jnp.mean(dxhat, -1, keepdims=True)
    m2 = jnp.mean(dxhat * xhat, -1, keepdims=True)
    return rstd * (dxhat - m1 - xhat * m2)


def allowed_cells(label_row):
    across = jnp.broadcast_to(label_row, (PAD, PAD))
    return across.T == across


def probabilities(q, k, bias_t, allowed):
    scores = nt(k, q) * SCALE + bias_t
    scores = jnp.where(allowed, scores, MASKED)
    weights = jnp.exp(scores - jnp.max(scores, 0, keepdims=True))
    return weights * (1.0 / jnp.sum(weights, 0, keepdims=True))


def score_grad(p, v, dc):
    dp = nt(v, dc)
    inner = jnp.sum(dp * p, 0, keepdims=True)
    return p * (dp - inner)


class Late:
    def __init__(self, copy, ref):
        self.copy, self.ref = copy, ref

    def __getitem__(self, index):
        if self.copy is not None:
            self.copy.wait()
            self.copy = None
        return self.ref[index]

    @property
    def shape(self):
        return self.ref.shape


def call(body, outs, *args, scratch=(), flops=200_000_000, scalars=0, late=(), mib=None, hbm_outs=()):
    late = tuple(range(scalars, len(args))) if late == "all" else late
    shapes = [jax.ShapeDtypeStruct(s, d) for s, d in outs]
    spaces = [pltpu.SMEM] * scalars + [pltpu.VMEM] * (len(args) - scalars)
    for i in late:
        spaces[i] = pltpu.HBM
    buffers = [pltpu.VMEM(args[i].shape, args[i].dtype) for i in late]
    if late:
        buffers.append(pltpu.SemaphoreType.DMA((len(late),)))

    def kernel(*refs):
        refs, spare = refs[: len(refs) - len(buffers)], refs[len(refs) - len(buffers) :]
        refs = list(refs)
        lates = []
        for n, i in enumerate(late):
            copy = pltpu.make_async_copy(refs[i], spare[n], spare[-1].at[n])
            copy.start()
            refs[i] = Late(copy, spare[n])
            lates.append(refs[i])
        body(*refs)
        for x in lates:
            assert x.copy is None

    return pl.pallas_call(
        kernel,
        out_shape=shapes,
        out_specs=[
            pl.BlockSpec(memory_space=pl.ANY if n in hbm_outs else pltpu.VMEM)
            for n in range(len(outs))
        ],
        in_specs=[pl.BlockSpec(memory_space=m) for m in spaces],
        scratch_shapes=list(scratch) + buffers,
        compiler_params=pltpu.CompilerParams(vmem_limit_bytes=(mib or (56 if late else 16)) * 1024 * 1024),
        cost_estimate=pl.CostEstimate(flops=flops, bytes_accessed=1_000_000, transcendentals=0),
    )(*args)


def fine_forward(
    f, hl, hn, hd, roll, gain, wqkv, wo, bias, lab, send,
    xr_o, xn_o, qkv_o, p_o, c_o, skip_o, b_o, l_o, d_o,
    table,
):
    src = jnp.concatenate([f[...], hl[0:80, :], hn[0:96, :], hd[0:32, :]], 0)
    xr = nn(roll[...], src)
    xr_o[...] = xr.astype(BF)
    xhat, _ = normalise(xr)
    xn = (xhat * gain[...]).astype(BF)
    xn_o[...] = xn
    qkv_o[...] = nn(xn, wqkv[...]).astype(BF)
    table[...] = jnp.zeros((8, PAD, 128), F32)
    for h in range(8):
        table[h, 0:CELLS, 0:CELLS] = bias[h].astype(F32)
    biases = [table[h, :, 0:PAD].T for h in range(8)]
    for w in range(4):
        allowed = allowed_cells(lab[w : w + 1, :])
        rows = slice(w * PAD, (w + 1) * PAD)
        for h in range(8):
            at = 192 * h
            q = qkv_o[rows, at : at + 64]
            k = qkv_o[rows, at + 64 : at + 128]
            v = qkv_o[rows, at + 128 : at + 192]
            p = probabilities(q, k, biases[h], allowed).astype(BF)
            p_o[w * 8 + h] = p
            c_o[rows, 64 * h : 64 * h + 64] = tn(p, v).astype(BF)
    skip = (xr + nn(c_o[...], wo[...])).astype(BF)
    skip_o[...] = skip
    pieces = nn(send[...], skip).astype(BF)
    b_o[...] = pieces[:64]
    l_o[...] = pieces[64:128]
    d_o[...] = pieces[128:]


def merge_forward(
    win, b, l, d, unroll, order, gain_m, wm, gain_c, send,
    skip_o, pat_o, mn_o, z_o, zn_o, b_o, l_o, d_o,
):
    src = jnp.concatenate([win[...], b[...], l[...], d[...]], 0)
    skip_o[...] = nn(unroll[...], src).astype(BF)
    cells = nn(order[...], src)
    patches = jnp.concatenate([cells[72 * k : 72 * k + 72] for k in range(4)], 1)
    pat_o[...] = patches.astype(BF)
    mhat, _ = normalise(patches)
    mn = (mhat * gain_m[...]).astype(BF)
    mn_o[...] = mn
    z = nn(mn, wm[...]).astype(BF)
    z_o[...] = z
    zhat, _ = normalise(z.astype(F32))
    zn = (zhat * gain_c[...]).astype(BF)
    zn_o[...] = zn
    pieces = nn(send[...], zn).astype(BF)
    b_o[...] = pieces[0:32]
    l_o[...] = pieces[32:64]
    d_o[...] = pieces[64:96]


def first_pieces(f, go, send, lat_o, lon_o, corner_o, tile_o):
    tile = jnp.concatenate([go[r].astype(F32) for r in range(6)], 0).astype(BF)
    tile_o[...] = tile
    pieces = nn(send[...], tile).astype(BF)
    fine = f[...]
    cells = fine.astype(F32).reshape(12, 24, 512)
    lat_o[0:80, :] = fine[0:80]
    lon_o[0:96, :] = cells[:, 0:8].reshape(96, 512).astype(BF)
    corner_o[0:32, :] = cells[0:4, 0:8].reshape(32, 512).astype(BF)
    for i, (o, at) in enumerate(((lat_o, 80), (lon_o, 96), (corner_o, 32))):
        o[at : at + 32, :] = pieces[32 * i : 32 * i + 32, 0:512]
        o[at + 32 : at + 64, :] = pieces[32 * i : 32 * i + 32, 512:]


def pack_weights(w, o, bias, out):
    out[0:192, :] = w[...]
    out[192:256, :] = o[...]
    out[256:272, :] = jnp.zeros((16, 1024), BF)
    for t in range(5):
        n = min(16, CELLS - 16 * t)
        rows = bias[0, 16 * t : 16 * t + n, :]
        out[256 : 256 + n, 128 * t : 128 * t + CELLS] = rows


def coarse_window(tile, b, l, d, own, far, out):
    src = jnp.concatenate([b[...], l[...], d[...]], 0)
    out[...] = (nn(own[...], tile[...]) + nn(far[...], src)).astype(BF)


def coarse_window_labelled(tile, b, l, d, own, far, lab, out):
    parts = []
    for r, at in ((b, 80), (l, 96), (d, 32)):
        parts.append(jnp.concatenate([r[at : at + 32, :], r[at + 32 : at + 64, :]], 1))
    rows = nn(own[...], tile[...]) + nn(far[...], jnp.concatenate(parts, 0))
    at = lax.broadcasted_iota(jnp.int32, rows.shape, 0)
    out[...] = jnp.where(at == CELLS, jnp.broadcast_to(lab[...], rows.shape), rows).astype(BF)


def coarse_attention(
    u0, u1, u2, u3, g0, g1, g2, g3, w0, w1, w2, w3,
    sd0, sd1, sd2, sd3, gw0, gw1, gw2, gw3,
    qkv, ctx, dqkv, bias_sum,
):
    ws = (w0, w1, w2, w3)
    u = jnp.concatenate([r[...] for r in (u0, u1, u2, u3)], 0)
    live = lax.broadcasted_iota(jnp.int32, (PAD, 1024), 0) < CELLS
    labels = []
    parts = []
    for r in (g0, g1, g2, g3):
        rows = r[...].astype(F32)
        labels.append(rows[CELLS : CELLS + 1, 0:PAD])
        parts.append(jnp.where(live, rows, 0.0).astype(BF))
    g = jnp.concatenate(parts, 0)
    wo = jnp.concatenate([r[192:256, :] for r in ws], 0)
    dc = nt(g, wo).astype(BF)
    for s in range(4):
        qkv[s] = nt(u, ws[s][0:192, :]).astype(BF)
    masks = [allowed_cells(row) for row in labels]
    for s in range(4):
        groups = [ws[s][256:272, 128 * t : 128 * t + PAD] for t in range(5)]
        bias = jnp.concatenate(groups, 0).astype(F32).T
        total = jnp.zeros((PAD, PAD), F32)
        for w in range(4):
            rows = slice(w * PAD, (w + 1) * PAD)
            q = qkv[s, rows, 0:64]
            k = qkv[s, rows, 64:128]
            v = qkv[s, rows, 128:192]
            p = probabilities(q, k, bias, masks[w])
            pb = p.astype(BF)
            ctx[rows, 64 * s : 64 * s + 64] = tn(pb, v).astype(BF)
            dch = dc[rows, 64 * s : 64 * s + 64]
            ds = score_grad(p, v, dch)
            total = total + ds
            dsb = ds.astype(BF)
            dqkv[s, rows, 0:64] = (tn(dsb, k) * SCALE).astype(BF)
            dqkv[s, rows, 64:128] = (nn(dsb, q) * SCALE).astype(BF)
            dqkv[s, rows, 128:192] = nn(pb, dch).astype(BF)
        bias_sum[s, :, 0:PAD] = total.T
    bias_sum[:, :, PAD:] = jnp.zeros((4, PAD, 128 - PAD), F32)
    c = ctx[...]
    out = nn(c, wo)
    du = nn(dqkv[0], w0[0:192, :])
    for s in range(1, 4):
        du = du + nn(dqkv[s], ws[s][0:192, :])
    for w, o in enumerate((sd0, sd1, sd2, sd3)):
        o[0:PAD, :] = out[w * PAD : (w + 1) * PAD].astype(BF)
        o[PAD : 2 * PAD, :] = du[w * PAD : (w + 1) * PAD].astype(BF)
    gwo = tn(c, g).astype(BF)
    for s, o in enumerate((gw0, gw1, gw2, gw3)):
        o[0:192, :] = tn(dqkv[s], u).astype(BF)
        o[192:256, :] = gwo[64 * s : 64 * s + 64]
        o[256:272, 640:] = jnp.zeros((16, 384), BF)
        for t in range(5):
            o[256:272, 128 * t : 128 * t + 128] = bias_sum[s, 16 * t : 16 * t + 16].astype(BF)


def coarse_sum(a0, a1, a2, a3, back, own_o, b_o, l_o, d_o):
    total = a0[...].astype(F32) + a1[...].astype(F32) + a2[...].astype(F32) + a3[...].astype(F32)
    total = total.astype(BF)
    own_o[...] = total
    s = nn(back[...], total[0:PAD]).astype(BF)
    du = nn(back[...], total[PAD:]).astype(BF)
    for i, o in enumerate((b_o, l_o, d_o)):
        o[0:32, :] = s[32 * i : 32 * i + 32]
        o[32:64, :] = du[32 * i : 32 * i + 32]


def merge_backward(
    at, z, go, own, b, l, d, uown, ufar, gain_c, pat, gain_m, wm, gskip, spread,
    dskip_o, top_o, side_o, corner_o, gg_m, gg_c, out_o, *dz_os,
):
    pieces = [b[...], l[...], d[...]]
    far_s = jnp.concatenate([x[0:32] for x in pieces], 0)
    far_d = jnp.concatenate([x[32:64] for x in pieces], 0)
    mix = own[...]
    dzn = nn(uown[...], mix[PAD:]) + nn(ufar[...], far_d)
    z32 = z[...].astype(F32)
    out_o[...] = (z32 + nn(uown[...], mix[0:PAD]) + nn(ufar[...], far_s)).astype(BF)
    zhat, rstd = normalise(z32)
    gg_c[...] = jnp.sum(dzn * zhat, 0, keepdims=True)
    dz = (go[...].astype(F32) + norm_back(dzn, gain_c[...], zhat, rstd)).astype(BF)
    table = dz_os[4]
    table[...] = dz
    for k in range(4):
        dz_os[k][...] = table[:, pl.ds(pl.multiple_of((at[0] + k) % 4 * 256, 256), 256)]
    dmn = nt(dz, wm[...])
    mhat, mrstd = normalise(pat[...].astype(F32))
    gg_m[...] = jnp.sum(dmn * mhat, 0, keepdims=True)
    dpat = norm_back(dmn, gain_m[...], mhat, mrstd).astype(BF)
    cells = jnp.concatenate([dpat[:, 512 * k : 512 * k + 512] for k in range(4)], 0)
    dskip = (gskip[...].astype(F32) + nn(spread[...], cells)).astype(BF)
    dskip_o[...] = dskip
    top_o[...] = dskip[0:80]
    cells = dskip.astype(F32).reshape(12, 24, 512)
    side_o[...] = cells[:, 0:8].reshape(96, 512).astype(BF)
    corner_o[...] = cells[0:4, 0:8].reshape(32, 512).astype(BF)


def fine_backward(
    core, f, hl, hn, hd, roll, gain, wqkv, wo, xr, xn, qkv, p_in, c, send, gg_m, gg_c,
    dx_o, b_o, l_o, d_o, keep_o, give_o,
    dqkv, bias_sum, pack_o, sems,
):
    src = jnp.concatenate([f[...], hl[...], hn[...], hd[...]], 0)
    g32 = nn(roll[...], src)
    g = g32.astype(BF)
    dc = nt(g, wo[...]).astype(BF)
    bias_sum[...] = jnp.zeros((8, PAD, 128), F32)
    for h in range(8):
        at = 192 * h
        total = jnp.zeros((PAD, PAD), F32)
        for w in range(4):
            rows = slice(w * PAD, (w + 1) * PAD)
            q = qkv[rows, at : at + 64]
            k = qkv[rows, at + 64 : at + 128]
            v = qkv[rows, at + 128 : at + 192]
            pb = p_in[w * 8 + h]
            dch = dc[rows, 64 * h : 64 * h + 64]
            ds = score_grad(pb.astype(F32), v, dch)
            total = total + ds
            dsb = ds.astype(BF)
            dqkv[rows, at : at + 64] = (tn(dsb, k) * SCALE).astype(BF)
            dqkv[rows, at + 64 : at + 128] = (nn(dsb, q) * SCALE).astype(BF)
            dqkv[rows, at + 128 : at + 192] = nn(pb, dch).astype(BF)
        bias_sum[h, :, 0:PAD] = total
    dproj = dqkv[...]
    du = nt(dproj, wqkv[...])
    xhat, rstd = normalise(xr[...].astype(F32))
    gg_f = jnp.sum(du * xhat, 0, keepdims=True)
    dx = (g32 + norm_back(du, gain[...], xhat, rstd)).astype(BF)
    dx_o[...] = dx
    pieces = nn(send[...], dx).astype(BF)
    b_o[...] = pieces[:64]
    l_o[...] = pieces[64:128]
    d_o[...] = pieces[128:]
    gq = tn(xn[...], dproj)
    for i in range(12):
        pack_o[32 * i : 32 * i + 32] = gq[:, 128 * i : 128 * i + 128].reshape(32, 16, 128).astype(BF)
    go = tn(c[...], g)
    for i in range(4):
        pack_o[384 + 32 * i : 416 + 32 * i] = (
            go[:, 128 * i : 128 * i + 128].reshape(32, 16, 128).astype(BF)
        )
    for h in range(8):
        pack_o[512 + 5 * h : 517 + 5 * h] = bias_sum[h].reshape(5, 16, 128).astype(BF)
    rows = [gg_f[:, 128 * i : 128 * i + 128] for i in range(4)]
    rows += [gg_m[:, 128 * i : 128 * i + 128] for i in range(16)]
    rows += [gg_c[:, 128 * i : 128 * i + 128] for i in range(8)]
    rows.append(jnp.zeros((4, 128), F32))
    pack_o[552:554] = jnp.concatenate(rows, 0).reshape(2, 16, 128).astype(BF)
    pack_o[554:PARTS] = jnp.zeros((PARTS - 554, 16, 128), BF)

    copies = [
        pltpu.make_async_copy(pack_o.at[pl.ds(start, HALF)], o, sems.at[n])
        for n, (o, start) in enumerate(
            ((keep_o, core[0] * HALF), (give_o, (1 - core[0]) * HALF))
        )
    ]
    for x in copies:
        x.start()
    for x in copies:
        x.wait()


def merge_weight_share(core, *refs):
    total = tn(refs[0][...], refs[4][...])
    for k in range(1, 4):
        total = total + tn(refs[k][...], refs[4 + k][...])
    keep_o, give_o = refs[8], refs[9]

    def halves(first, second):
        first[0:64, :] = total[0:64].astype(BF)
        second[0:64, :] = total[64:128].astype(BF)
        first[64:128, :] = total[128:192].astype(BF)
        second[64:128, :] = total[192:256].astype(BF)

    @pl.when(core[0] == 0)
    def _():
        halves(keep_o, give_o)

    @pl.when(core[0] != 0)
    def _():
        halves(give_o, keep_o)


def pack_sums(at, g0, r0, g2, r2, keep, got, out):
    for a, (g, r) in ((at[0], (g0, r0)), (1 - at[0], (g2, r2))):
        head = (g[...].astype(F32) + r[...].astype(F32)).astype(BF)
        for j in range(8):
            row = pl.multiple_of(a * 3200 + 400 * j, 16)
            out[pl.ds(row, 272), :] = head[:, 128 * j : 128 * j + 128]
    merge = keep[...].astype(F32) + got[...].astype(F32)
    for q in range(16):
        rows = merge[8 * q : 8 * q + 8]
        for t in range(8):
            pair = [rows[:, 256 * t : 256 * t + 128], rows[:, 256 * t + 128 : 256 * t + 256]]
            row = 400 * q + 272 + 16 * t
            out[row : row + 16, :] = jnp.concatenate(pair, 0).astype(BF)


def unpack_sums(parts, strip_o, merge_o):
    total = parts[0:400, :].astype(F32)
    for q in range(1, 16):
        total = total + parts[400 * q : 400 * q + 400, :].astype(F32)
    strip_o[...] = total[0:272].astype(BF)
    for t in range(16):
        merge_o[:, 128 * t : 128 * t + 128] = total[272 + 8 * t : 280 + 8 * t]


def coarse_join(lon, *refs):
    parts, (gw_o, go_o, gb_o, table) = refs[:8], refs[8:]
    for k in range(8):
        at = pl.multiple_of((lon[0] + k) % 8 * 128, 128)
        gw_o[:, pl.ds(at, 128)] = parts[k][0:192, :].astype(F32)
        go_o[:, pl.ds(at, 128)] = parts[k][192:256, :].astype(F32)
        table[:, pl.ds(at, 128)] = parts[k][256:272, :].astype(F32)
    for t in range(5):
        n = min(16, CELLS - 16 * t)
        gb_o[0, 16 * t : 16 * t + n, :] = table[0:n, 128 * t : 128 * t + CELLS]


def fine_place(win, b, l, d, unroll, out):
    src = jnp.concatenate([win[...], b[...], l[...], d[...]], 0)
    out[...] = nn(unroll[...], src).astype(BF)


def sum_and_copy(parts, out):
    total = parts[0:5].astype(F32)
    for k in range(1, 64):
        total = total + parts[5 * k : 5 * k + 5].astype(F32)
    total = total.astype(BF)
    for k in range(64):
        out[5 * k : 5 * k + 5] = total


def unpack(core, mine, other, gq_o, gb_o, go_o, gain_o, pack):
    @pl.when(core[0] == 0)
    def _():
        pack[0:HALF] = mine[...]
        pack[HALF:PARTS] = other[...]

    @pl.when(core[0] != 0)
    def _():
        pack[0:HALF] = other[...]
        pack[HALF:PARTS] = mine[...]

    for i in range(12):
        gq_o[:, 128 * i : 128 * i + 128] = (
            pack[32 * i : 32 * i + 32].astype(F32).reshape(512, 128)
        )
    for i in range(4):
        go_o[:, 128 * i : 128 * i + 128] = (
            pack[384 + 32 * i : 416 + 32 * i].astype(F32).reshape(512, 128)
        )
    for h in range(8):
        t = pack[512 + 5 * h : 517 + 5 * h].astype(F32).reshape(80, 128)
        gb_o[h] = t[:, 0:PAD].T[0:CELLS, 0:CELLS]
    gain_o[...] = pack[552:554].astype(F32).reshape(32, 128)


def count_of(axes):
    n = 1
    for a in axes:
        n *= lax.axis_size(a)
    return n


def shift(x, axes, by):
    n = count_of(axes)
    return lax.ppermute(x, axes, [(i, (i + by) % n) for i in range(n)])


def shift_both(x, by):
    nl, nn_ = count_of(LAT), count_of(LON)
    pairs = [
        (i * nn_ + j, ((i + by) % nl) * nn_ + (j + by) % nn_)
        for i in range(nl)
        for j in range(nn_)
    ]
    return lax.ppermute(x, ALL, pairs)


def exchange(pieces, by):
    lat_piece, lon_piece, corner = pieces
    return shift(lat_piece, LAT, by), shift(lon_piece, LON, by), shift_both(corner, by)


def along_y(x):
    return [x] + [shift(x, ("y",), -k) for k in (1, 2, 3)]


def gather_along_lon(x):
    return [x] + [shift(x, LON, -k) for k in range(1, 8)]


def back_along_y(parts):
    return [parts[0]] + [shift(parts[k], ("y",), k) for k in (1, 2, 3)]


def after(x, *others):
    return lax.optimization_barrier((x, others))[0]


def local(
    fields,
    region_fine,
    region_coarse,
    gain_fine,
    qkv_fine,
    bias_fine,
    out_fine,
    gain_merge,
    merge_weight,
    gain_coarse,
    qkv_coarse,
    bias_coarse,
    out_coarse,
    grad_skip,
    grad_out,
):
    c_roll, c_send, c_unroll = make_fine_roll(), make_fine_send(), make_fine_unroll()
    roll_own, roll_far = make_coarse_roll()
    back_own, back_far = make_coarse_unroll()
    roll_f, send_f, unroll_f = const(c_roll), const(c_send), const(c_unroll)
    order_f = const(c_unroll[patch_order()])
    spread = np.zeros((288, 288), np.float32)
    spread[patch_order(), np.arange(288)] = 1
    spread_f = const(spread)
    send_c, back_c = const(make_coarse_send()), const(make_coarse_back())
    roll_own, roll_far = const(roll_own), const(roll_far)
    back_own, back_far = const(back_own), const(back_far)
    gain_f2, gain_m2, gain_c2 = gain_fine[None], gain_merge[None], gain_coarse[None]

    core = lax.axis_index("c").astype(jnp.int32).reshape(1)
    tile = fields.reshape(288, 512)
    piece = ((32, 1024), BF)
    win = ((320, 512), BF)
    window = ((PAD, 1024), BF)

    *first, go_tile = call(
        first_pieces,
        [((144, 512), BF), ((160, 512), BF), ((96, 512), BF), ((72, 1024), BF)],
        tile, grad_out, send_c,
        late="all",
    )
    first_far = exchange(first, -1)

    (w0,) = call(pack_weights, [((272, 1024), BF)], qkv_coarse.T, out_coarse, bias_coarse)
    w2 = shift(w0, ("xh",), 1)
    w1 = shift(w0, ("c",), 1)

    label_c = jnp.pad(
        region_coarse.reshape(1, 72).astype(F32), ((0, 0), (0, 952)), constant_values=-1.0
    )
    label_f = region_fine.reshape(2, 6, 2, 12).transpose(0, 2, 1, 3).reshape(4, 72).astype(F32)
    label_f = jnp.pad(label_f, ((0, 0), (0, 8)), constant_values=-1.0)

    (gw_win,) = call(
        coarse_window_labelled, [window], go_tile, *first_far, roll_own, roll_far, label_c
    )
    g_all = along_y(gw_win)
    xr, xn, qkv, prob, ctx, skip_win, *skip_pieces = call(
        fine_forward,
        [win, win, ((320, 1536), BF), ((32, PAD, PAD), BF), win, win,
         ((64, 512), BF), ((64, 512), BF), ((32, 512), BF)],
        after(tile, gw_win), *first_far, roll_f, gain_f2, qkv_fine, out_fine, bias_fine, label_f, send_f,
        late="all",
        scratch=[pltpu.VMEM((8, PAD, 128), F32)],
        flops=3_000_000_000,
    )
    s_far = exchange(skip_pieces, 1)
    skip_win = after(skip_win, g_all)
    skip_level, pat, mn, z, zn, *z_pieces = call(
        merge_forward,
        [((288, 512), BF), ((72, 2048), BF), ((72, 2048), BF), ((72, 1024), BF), ((72, 1024), BF),
         piece, piece, piece],
        skip_win, *s_far, unroll_f, order_f, gain_m2, merge_weight, gain_c2, send_c,
        late="all",
        flops=2_500_000_000,
    )
    z_far = exchange(z_pieces, -1)
    (u_win,) = call(coarse_window, [window], zn, *z_far, roll_own, roll_far)
    w3 = shift(after(w2, u_win), ("c",), 1)
    u_all = along_y(u_win)
    outs = call(
        coarse_attention,
        [((2 * PAD, 1024), BF)] * 4 + [((272, 1024), BF)] * 4,
        *u_all, *g_all, w0, w1, w2, w3,
        late="all",
        scratch=[
            pltpu.VMEM((4, 320, 192), BF), pltpu.VMEM((320, 256), BF),
            pltpu.VMEM((4, 320, 192), BF), pltpu.VMEM((4, PAD, 128), F32),
        ],
        flops=9_000_000_000,
    )
    gw0, gw1, gw2, gw3 = outs[4:]
    du_parts = back_along_y(outs[0:4])
    r0 = shift(gw1, ("c",), 1)
    r2 = shift(gw3, ("c",), 1)
    du_parts[0] = after(du_parts[0], r0, r2)
    du_win, *du_pieces = call(
        coarse_sum, [((2 * PAD, 1024), BF)] + [((64, 1024), BF)] * 3, *du_parts, back_c
    )
    du_far = exchange(du_pieces, 1)
    at_y = lax.axis_index("y").astype(jnp.int32).reshape(1)
    dskip, k_lat, k_lon, k_corner, gg_m, gg_c, output, *dz_parts = call(
        merge_backward,
        [((288, 512), BF), ((80, 512), BF), ((96, 512), BF), ((32, 512), BF),
         ((1, 2048), F32), ((1, 1024), F32), ((72, 1024), BF)] + [((72, 256), BF)] * 4,
        at_y, z, go_tile, du_win, *du_far, back_own, back_far, gain_c2, pat, gain_m2, merge_weight,
        grad_skip.reshape(288, 512), spread_f,
        scratch=[pltpu.VMEM((72, 1024), BF)],
        scalars=1,
        late="all",
        flops=3_000_000_000,
    )
    k_far = exchange((k_lat, k_lon, k_corner), -1)
    mn_own = after(mn, du_win)
    mn_all = [mn_own] + [shift(mn_own, ("y",), k) for k in (1, 2, 3)]
    dz_all = dz_parts[0:1] + [shift(dz_parts[k], ("y",), k) for k in (1, 2, 3)]
    merge_keep, merge_give = call(
        merge_weight_share, [((128, 2048), BF)] * 2, core, *dz_all, *mn_all, scalars=1, late="all"
    )
    merge_got = shift(merge_give, ("c",), 1)
    xh = lax.axis_index("xh").astype(jnp.int32).reshape(1)
    (packed,) = call(
        pack_sums, [((6400, 128), BF)], xh, gw0, r0, gw2, r2, merge_keep, merge_got, scalars=1
    )
    packed = after(packed, k_far)
    sums = lax.all_to_all(packed, ("xh",) + LON, 0, 0, tiled=True)
    dskip = after(dskip, packed)
    dx_win, d_lat, d_lon, d_corner, keep, give = call(
        fine_backward,
        [win, ((64, 512), BF), ((64, 512), BF), ((32, 512), BF),
         ((HALF, 16, 128), BF), ((HALF, 16, 128), BF)],
        core, dskip, *k_far, roll_f, gain_f2, qkv_fine, out_fine, xr, xn, qkv, prob, ctx, send_f,
        gg_m, gg_c,
        late="all",
        scratch=[
            pltpu.VMEM((320, 1536), BF), pltpu.VMEM((8, PAD, 128), F32),
            pltpu.VMEM((PARTS, 16, 128), BF), pltpu.SemaphoreType.DMA((2,)),
        ],
        scalars=1,
        hbm_outs=(4, 5),
        flops=1_000_000,
    )


    strip, merge_t = call(unpack_sums, [((272, 128), BF), ((8, 2048), F32)], sums)
    lon = lax.axis_index(LON).astype(jnp.int32).reshape(1)

    keep = after(keep, sums)
    half = (keep.astype(F32) + shift(give, ("c",), 1).astype(F32)).astype(BF)
    spread_out = lax.all_to_all(half, CHIPS, 0, 0, tiled=True)
    gw_c, go_c, gb_c = call(
        coarse_join, [((192, 1024), F32), ((64, 1024), F32), ((1, CELLS, CELLS), F32)],
        lon, *gather_along_lon(strip),
        scratch=[pltpu.VMEM((16, 1024), F32)], scalars=1,
    )
    (copies,) = call(sum_and_copy, [((HALF, 16, 128), BF)], spread_out)
    copies = after(copies, gw_c)
    whole_half = lax.all_to_all(copies, CHIPS, 0, 0, tiled=True)
    d_far = exchange(after((d_lat, d_lon, d_corner), copies), 1)
    (grad_fields,) = call(fine_place, [((288, 512), BF)], dx_win, *d_far, unroll_f)
    whole_half = after(whole_half, merge_t, grad_fields)
    other_half = shift(whole_half, ("c",), 1)

    gq, gb, go, gains = call(
        unpack,
        [((512, 1536), F32), ((8, CELLS, CELLS), F32), ((512, 512), F32), ((32, 128), F32)],
        core, whole_half, other_half,
        scratch=[pltpu.VMEM((PARTS, 16, 128), BF)],
        scalars=1,
    )
    return (
        skip_level.reshape(12, 24, 512),
        output.reshape(6, 12, 1024),
        grad_fields.reshape(12, 24, 512),
        gains[0:4].reshape(512),
        gq,
        gb,
        go,
        gains[4:20].reshape(2048),
        merge_t.T,
        gains[20:28].reshape(1024),
        gw_c.T,
        gb_c,
        go_c,
    )


def solution(mesh):
    fine_mesh = Mesh(mesh.devices.reshape(4, 2, 2, 4, 2), ALL)
    grid = P(LAT, LON, None)
    placed = (
        grid,
        P(LAT, LON),
        P(LAT, LON),
        P(),
        P(),
        P(),
        P(),
        P(),
        P(),
        P(),
        P(None, LAT),
        P(LAT, None, None),
        P(LAT, None),
        grid,
        grid,
    )
    return jax.shard_map(
        local,
        mesh=fine_mesh,
        in_specs=placed,
        out_specs=(
            grid,
            grid,
            grid,
            P(),
            P(),
            P(),
            P(),
            P(),
            P(None, ALL),
            P(),
            P(None, LAT),
            P(LAT, None, None),
            P(LAT, None),
        ),
        check_vma=False,
    )
```

```python
import jax
import jax.numpy as jnp
import numpy as np
from jax import lax
from jax.experimental import pallas as pl
from jax.experimental.pallas import tpu as pltpu
from jax.sharding import Mesh
from jax.sharding import PartitionSpec as P

EPSILON = 1e-05
MASKED = -1000000000.0
BF = jnp.bfloat16
F32 = jnp.float32
CELLS = 72
PAD = 80
SCALE = 0.125

LAT = ("y", "xh", "c")
LON = ("z", "xl")
ALL = LAT + LON
CHIPS = ("y", "xh", "z", "xl")
HALF = 288
PARTS = 576


def fine_window_row(rr, cc):
    return (rr // 6 * 2 + cc // 12) * PAD + (rr % 6) * 12 + cc % 12


def make_fine_roll():
    m = np.zeros((320, 496), np.float32)
    for rr in range(12):
        for cc in range(24):
            if rr < 9 and cc < 18:
                s = (rr + 3) * 24 + cc + 6
            elif cc < 18:
                s = 288 + (rr - 9) * 24 + cc + 6
            elif rr < 9:
                s = 368 + (rr + 3) * 8 + cc - 18
            else:
                s = 464 + (rr - 9) * 8 + cc - 18
            m[fine_window_row(rr, cc), s] = 1
    return m


def make_fine_send():
    m = np.zeros((160, 320), np.float32)
    for r in range(3):
        for cc in range(18):
            m[r * 18 + cc, fine_window_row(9 + r, cc)] = 1
    for rr in range(9):
        for q in range(6):
            m[64 + rr * 6 + q, fine_window_row(rr, 18 + q)] = 1
    for r in range(3):
        for q in range(6):
            m[128 + r * 6 + q, fine_window_row(9 + r, 18 + q)] = 1
    return m


def make_fine_unroll():
    m = np.zeros((288, 480), np.float32)
    for r in range(12):
        for c in range(24):
            if r >= 3 and c >= 6:
                s = fine_window_row(r - 3, c - 6)
            elif c >= 6:
                s = 320 + r * 18 + c - 6
            elif r >= 3:
                s = 384 + (r - 3) * 6 + c
            else:
                s = 448 + r * 6 + c
            m[r * 24 + c, s] = 1
    return m


def patch_order():
    order = []
    for ro in range(2):
        for co in range(2):
            for r in range(6):
                for c in range(12):
                    order.append((2 * r + ro) * 24 + 2 * c + co)
    return np.array(order)


def make_coarse_send():
    m = np.zeros((96, 72), np.float32)
    for r in range(3):
        for c in range(6):
            m[r * 6 + c, r * 12 + c + 6] = 1
            m[32 + r * 6 + c, (r + 3) * 12 + c] = 1
            m[64 + r * 6 + c, r * 12 + c] = 1
    return m


def make_coarse_roll():
    own = np.zeros((PAD, 72), np.float32)
    far = np.zeros((PAD, 96), np.float32)
    for a in range(6):
        for b in range(12):
            row = a * 12 + b
            if a < 3 and b < 6:
                own[row, (a + 3) * 12 + b + 6] = 1
            elif b < 6:
                far[row, (a - 3) * 6 + b] = 1
            elif a < 3:
                far[row, 32 + a * 6 + b - 6] = 1
            else:
                far[row, 64 + (a - 3) * 6 + b - 6] = 1
    return own, far


def make_coarse_back():
    m = np.zeros((96, PAD), np.float32)
    for r in range(3):
        for c in range(6):
            m[r * 6 + c, (r + 3) * 12 + c] = 1
            m[32 + r * 6 + c, r * 12 + c + 6] = 1
            m[64 + r * 6 + c, (r + 3) * 12 + c + 6] = 1
    return m


def make_coarse_unroll():
    own = np.zeros((72, PAD), np.float32)
    far = np.zeros((72, 96), np.float32)
    for r in range(6):
        for c in range(12):
            row = r * 12 + c
            if r >= 3 and c >= 6:
                own[row, (r - 3) * 12 + c - 6] = 1
            elif c >= 6:
                far[row, r * 6 + c - 6] = 1
            elif r >= 3:
                far[row, 32 + (r - 3) * 6 + c] = 1
            else:
                far[row, 64 + r * 6 + c] = 1
    return own, far


def const(m):
    return jnp.asarray(np.asarray(m, np.float32), BF)


def nn(a, b):
    return lax.dot_general(a, b, (((1,), (0,)), ((), ())), preferred_element_type=F32)


def nt(a, b):
    return lax.dot_general(a, b, (((1,), (1,)), ((), ())), preferred_element_type=F32)


def tn(a, b):
    return lax.dot_general(a, b, (((0,), (0,)), ((), ())), preferred_element_type=F32)


def normalise(x):
    average = jnp.mean(x, -1, keepdims=True)
    centred = x - average
    rstd = lax.rsqrt(jnp.mean(centred * centred, -1, keepdims=True) + EPSILON)
    return centred * rstd, rstd


def norm_back(dy, gain, xhat, rstd):
    dxhat = dy * gain
    m1 = jnp.mean(dxhat, -1, keepdims=True)
    m2 = jnp.mean(dxhat * xhat, -1, keepdims=True)
    return rstd * (dxhat - m1 - xhat * m2)


def allowed_cells(label_row):
    across = jnp.broadcast_to(label_row, (PAD, PAD))
    return across.T == across


def probabilities(q, k, bias_t, allowed):
    scores = nt(k, q) * SCALE + bias_t
    scores = jnp.where(allowed, scores, MASKED)
    weights = jnp.exp(scores - jnp.max(scores, 0, keepdims=True))
    return weights * (1.0 / jnp.sum(weights, 0, keepdims=True))


def score_grad(p, v, dc):
    dp = nt(v, dc)
    inner = jnp.sum(dp * p, 0, keepdims=True)
    return p * (dp - inner)


class Late:
    def __init__(self, copy, ref):
        self.copy, self.ref = copy, ref

    def __getitem__(self, index):
        if self.copy is not None:
            self.copy.wait()
            self.copy = None
        return self.ref[index]

    @property
    def shape(self):
        return self.ref.shape


def call(body, outs, *args, scratch=(), flops=200_000_000, scalars=0, late=(), mib=None, hbm_outs=()):
    late = tuple(range(scalars, len(args))) if late == "all" else late
    shapes = [jax.ShapeDtypeStruct(s, d) for s, d in outs]
    spaces = [pltpu.SMEM] * scalars + [pltpu.VMEM] * (len(args) - scalars)
    for i in late:
        spaces[i] = pl.ANY
    buffers = [pltpu.VMEM(args[i].shape, args[i].dtype) for i in late]
    if late:
        buffers.append(pltpu.SemaphoreType.DMA((len(late),)))

    def kernel(*refs):
        refs, spare = refs[: len(refs) - len(buffers)], refs[len(refs) - len(buffers) :]
        refs = list(refs)
        lates = []
        for n, i in enumerate(late):
            copy = pltpu.make_async_copy(refs[i], spare[n], spare[-1].at[n])
            copy.start()
            refs[i] = Late(copy, spare[n])
            lates.append(refs[i])
        body(*refs)
        for x in lates:
            assert x.copy is None

    return pl.pallas_call(
        kernel,
        out_shape=shapes,
        out_specs=[
            pl.BlockSpec(memory_space=pl.ANY if n in hbm_outs else pltpu.VMEM)
            for n in range(len(outs))
        ],
        in_specs=[pl.BlockSpec(memory_space=m) for m in spaces],
        scratch_shapes=list(scratch) + buffers,
        compiler_params=pltpu.CompilerParams(vmem_limit_bytes=(mib or (56 if late else 16)) * 1024 * 1024),
        cost_estimate=pl.CostEstimate(flops=flops, bytes_accessed=1_000_000, transcendentals=0),
    )(*args)


def fine_forward(
    f, hl, hn, hd, roll, gain, wqkv, wo, bias, lab, send,
    xr_o, xn_o, qkv_o, p_o, c_o, skip_o, b_o, l_o, d_o,
    table,
):
    src = jnp.concatenate([f[...], hl[0:80, :], hn[0:96, :], hd[0:32, :]], 0)
    xr = nn(roll[...], src)
    xr_o[...] = xr.astype(BF)
    xhat, _ = normalise(xr)
    xn = (xhat * gain[...]).astype(BF)
    xn_o[...] = xn
    qkv_o[...] = nn(xn, wqkv[...]).astype(BF)
    table[...] = jnp.zeros((8, PAD, 128), F32)
    for h in range(8):
        table[h, 0:CELLS, 0:CELLS] = bias[h].astype(F32)
    biases = [table[h, :, 0:PAD].T for h in range(8)]
    for w in range(4):
        allowed = allowed_cells(lab[w : w + 1, :])
        rows = slice(w * PAD, (w + 1) * PAD)
        for h in range(8):
            at = 192 * h
            q = qkv_o[rows, at : at + 64]
            k = qkv_o[rows, at + 64 : at + 128]
            v = qkv_o[rows, at + 128 : at + 192]
            p = probabilities(q, k, biases[h], allowed).astype(BF)
            p_o[w * 8 + h] = p
            c_o[rows, 64 * h : 64 * h + 64] = tn(p, v).astype(BF)
    skip = (xr + nn(c_o[...], wo[...])).astype(BF)
    skip_o[...] = skip
    pieces = nn(send[...], skip).astype(BF)
    b_o[...] = pieces[:64]
    l_o[...] = pieces[64:128]
    d_o[...] = pieces[128:]


def merge_forward(
    win, b, l, d, unroll, order, gain_m, wm, gain_c, send,
    skip_o, pat_o, mn_o, z_o, zn_o, b_o, l_o, d_o,
):
    src = jnp.concatenate([win[...], b[...], l[...], d[...]], 0)
    skip_o[...] = nn(unroll[...], src).astype(BF)
    cells = nn(order[...], src)
    patches = jnp.concatenate([cells[72 * k : 72 * k + 72] for k in range(4)], 1)
    pat_o[...] = patches.astype(BF)
    mhat, _ = normalise(patches)
    mn = (mhat * gain_m[...]).astype(BF)
    mn_o[...] = mn
    z = nn(mn, wm[...]).astype(BF)
    z_o[...] = z
    zhat, _ = normalise(z.astype(F32))
    zn = (zhat * gain_c[...]).astype(BF)
    zn_o[...] = zn
    pieces = nn(send[...], zn).astype(BF)
    b_o[...] = pieces[0:32]
    l_o[...] = pieces[32:64]
    d_o[...] = pieces[64:96]


def first_pieces(f, go, send, lat_o, lon_o, corner_o, tile_o):
    tile = jnp.concatenate([go[r].astype(F32) for r in range(6)], 0).astype(BF)
    tile_o[...] = tile
    pieces = nn(send[...], tile).astype(BF)
    fine = f[...]
    cells = fine.astype(F32).reshape(12, 24, 512)
    lat_o[0:80, :] = fine[0:80]
    lon_o[0:96, :] = cells[:, 0:8].reshape(96, 512).astype(BF)
    corner_o[0:32, :] = cells[0:4, 0:8].reshape(32, 512).astype(BF)
    for i, (o, at) in enumerate(((lat_o, 80), (lon_o, 96), (corner_o, 32))):
        o[at : at + 32, :] = pieces[32 * i : 32 * i + 32, 0:512]
        o[at + 32 : at + 64, :] = pieces[32 * i : 32 * i + 32, 512:]


def pack_weights(w, o, bias, out):
    out[0:192, :] = w[...]
    out[192:256, :] = o[...]
    out[256:272, :] = jnp.zeros((16, 1024), BF)
    for t in range(5):
        n = min(16, CELLS - 16 * t)
        rows = bias[0, 16 * t : 16 * t + n, :]
        out[256 : 256 + n, 128 * t : 128 * t + CELLS] = rows


def coarse_window(tile, b, l, d, own, far, out):
    src = jnp.concatenate([b[...], l[...], d[...]], 0)
    out[...] = (nn(own[...], tile[...]) + nn(far[...], src)).astype(BF)


def coarse_window_labelled(tile, b, l, d, own, far, lab, out):
    parts = []
    for r, at in ((b, 80), (l, 96), (d, 32)):
        parts.append(jnp.concatenate([r[at : at + 32, :], r[at + 32 : at + 64, :]], 1))
    rows = nn(own[...], tile[...]) + nn(far[...], jnp.concatenate(parts, 0))
    at = lax.broadcasted_iota(jnp.int32, rows.shape, 0)
    out[...] = jnp.where(at == CELLS, jnp.broadcast_to(lab[...], rows.shape), rows).astype(BF)


def coarse_attention(
    u0, u1, u2, u3, g0, g1, g2, g3, w0, w1, w2, w3,
    d0, d1, d2, d3, s0, s1, s2, s3, gw0, gw1, gw2, gw3,
    qkv, ctx, dqkv, bias_sum,
):
    ws = (w0, w1, w2, w3)
    u = jnp.concatenate([r[...] for r in (u0, u1, u2, u3)], 0)
    live = lax.broadcasted_iota(jnp.int32, (PAD, 1024), 0) < CELLS
    labels = []
    parts = []
    for r in (g0, g1, g2, g3):
        rows = r[...].astype(F32)
        labels.append(rows[CELLS : CELLS + 1, 0:PAD])
        parts.append(jnp.where(live, rows, 0.0).astype(BF))
    g = jnp.concatenate(parts, 0)
    wo = jnp.concatenate([r[192:256, :] for r in ws], 0)
    dc = nt(g, wo).astype(BF)
    for s in range(4):
        qkv[s] = nt(u, ws[s][0:192, :]).astype(BF)
    masks = [allowed_cells(row) for row in labels]
    for s in range(4):
        groups = [ws[s][256:272, 128 * t : 128 * t + PAD] for t in range(5)]
        bias = jnp.concatenate(groups, 0).astype(F32).T
        total = jnp.zeros((PAD, PAD), F32)
        for w in range(4):
            rows = slice(w * PAD, (w + 1) * PAD)
            q = qkv[s, rows, 0:64]
            k = qkv[s, rows, 64:128]
            v = qkv[s, rows, 128:192]
            p = probabilities(q, k, bias, masks[w])
            pb = p.astype(BF)
            ctx[rows, 64 * s : 64 * s + 64] = tn(pb, v).astype(BF)
            dch = dc[rows, 64 * s : 64 * s + 64]
            ds = score_grad(p, v, dch)
            total = total + ds
            dsb = ds.astype(BF)
            dqkv[s, rows, 0:64] = (tn(dsb, k) * SCALE).astype(BF)
            dqkv[s, rows, 64:128] = (nn(dsb, q) * SCALE).astype(BF)
            dqkv[s, rows, 128:192] = nn(pb, dch).astype(BF)
        bias_sum[s, :, 0:PAD] = total.T
    bias_sum[:, :, PAD:] = jnp.zeros((4, PAD, 128 - PAD), F32)
    c = ctx[...]
    out = nn(c, wo)
    du = nn(dqkv[0], w0[0:192, :])
    for s in range(1, 4):
        du = du + nn(dqkv[s], ws[s][0:192, :])
    for w, (do, so) in enumerate(((d0, s0), (d1, s1), (d2, s2), (d3, s3))):
        do[...] = du[w * PAD : (w + 1) * PAD].astype(BF)
        so[...] = out[w * PAD : (w + 1) * PAD].astype(BF)
    gwo = tn(c, g).astype(BF)
    for s, o in enumerate((gw0, gw1, gw2, gw3)):
        o[0:192, :] = tn(dqkv[s], u).astype(BF)
        o[192:256, :] = gwo[64 * s : 64 * s + 64]
        o[256:272, 640:] = jnp.zeros((16, 384), BF)
        for t in range(5):
            o[256:272, 128 * t : 128 * t + 128] = bias_sum[s, 16 * t : 16 * t + 16].astype(BF)


def coarse_sum(a0, a1, a2, a3, back, own_o, b_o, l_o, d_o):
    total = a0[...].astype(F32) + a1[...].astype(F32) + a2[...].astype(F32) + a3[...].astype(F32)
    total = total.astype(BF)
    own_o[...] = total
    pieces = nn(back[...], total).astype(BF)
    b_o[...] = pieces[0:32]
    l_o[...] = pieces[32:64]
    d_o[...] = pieces[64:96]


def coarse_output(z, own, b, l, d, uown, ufar, out_o):
    far = jnp.concatenate([b[...], l[...], d[...]], 0)
    s = nn(uown[...], own[...]) + nn(ufar[...], far)
    rows = z[...].astype(F32) + s
    for r in range(6):
        out_o[r] = rows[12 * r : 12 * r + 12].astype(BF)


def merge_backward(
    at, z, go, own, b, l, d, uown, ufar, gain_c, pat, gain_m, wm, gskip, spread,
    dskip_o, top_o, side_o, corner_o, gg_m, gg_c, *dz_os,
):
    far = jnp.concatenate([b[...], l[...], d[...]], 0)
    dzn = nn(uown[...], own[...]) + nn(ufar[...], far)
    z32 = z[...].astype(F32)
    zhat, rstd = normalise(z32)
    gg_c[...] = jnp.sum(dzn * zhat, 0, keepdims=True)
    dz = (go[...].astype(F32) + norm_back(dzn, gain_c[...], zhat, rstd)).astype(BF)
    table = dz_os[4]
    table[...] = dz
    for k in range(4):
        dz_os[k][...] = table[:, pl.ds(pl.multiple_of((at[0] + k) % 4 * 256, 256), 256)]
    dmn = nt(dz, wm[...])
    mhat, mrstd = normalise(pat[...].astype(F32))
    gg_m[...] = jnp.sum(dmn * mhat, 0, keepdims=True)
    dpat = norm_back(dmn, gain_m[...], mhat, mrstd).astype(BF)
    cells = jnp.concatenate([dpat[:, 512 * k : 512 * k + 512] for k in range(4)], 0)
    dskip = (gskip[...].astype(F32) + nn(spread[...], cells)).astype(BF)
    dskip_o[...] = dskip
    top_o[...] = dskip[0:80]
    cells = dskip.astype(F32).reshape(12, 24, 512)
    side_o[...] = cells[:, 0:8].reshape(96, 512).astype(BF)
    corner_o[...] = cells[0:4, 0:8].reshape(32, 512).astype(BF)


def fine_backward(
    core, f, hl, hn, hd, roll, gain, wqkv, wo, xr, xn, qkv, p_in, c, send, gg_m, gg_c,
    dx_o, b_o, l_o, d_o, keep_o, give_o,
    dqkv, bias_sum, pack_o, sems,
):
    src = jnp.concatenate([f[...], hl[...], hn[...], hd[...]], 0)
    g32 = nn(roll[...], src)
    g = g32.astype(BF)
    dc = nt(g, wo[...]).astype(BF)
    bias_sum[...] = jnp.zeros((8, PAD, 128), F32)
    for h in range(8):
        at = 192 * h
        total = jnp.zeros((PAD, PAD), F32)
        for w in range(4):
            rows = slice(w * PAD, (w + 1) * PAD)
            q = qkv[rows, at : at + 64]
            k = qkv[rows, at + 64 : at + 128]
            v = qkv[rows, at + 128 : at + 192]
            pb = p_in[w * 8 + h]
            dch = dc[rows, 64 * h : 64 * h + 64]
            ds = score_grad(pb.astype(F32), v, dch)
            total = total + ds
            dsb = ds.astype(BF)
            dqkv[rows, at : at + 64] = (tn(dsb, k) * SCALE).astype(BF)
            dqkv[rows, at + 64 : at + 128] = (nn(dsb, q) * SCALE).astype(BF)
            dqkv[rows, at + 128 : at + 192] = nn(pb, dch).astype(BF)
        bias_sum[h, :, 0:PAD] = total
    dproj = dqkv[...]
    du = nt(dproj, wqkv[...])
    xhat, rstd = normalise(xr[...].astype(F32))
    gg_f = jnp.sum(du * xhat, 0, keepdims=True)
    dx = (g32 + norm_back(du, gain[...], xhat, rstd)).astype(BF)
    dx_o[...] = dx
    pieces = nn(send[...], dx).astype(BF)
    b_o[...] = pieces[:64]
    l_o[...] = pieces[64:128]
    d_o[...] = pieces[128:]
    gq = tn(xn[...], dproj)
    for i in range(12):
        pack_o[32 * i : 32 * i + 32] = gq[:, 128 * i : 128 * i + 128].reshape(32, 16, 128).astype(BF)
    go = tn(c[...], g)
    for i in range(4):
        pack_o[384 + 32 * i : 416 + 32 * i] = (
            go[:, 128 * i : 128 * i + 128].reshape(32, 16, 128).astype(BF)
        )
    for h in range(8):
        pack_o[512 + 5 * h : 517 + 5 * h] = bias_sum[h].reshape(5, 16, 128).astype(BF)
    rows = [gg_f[:, 128 * i : 128 * i + 128] for i in range(4)]
    rows += [gg_m[:, 128 * i : 128 * i + 128] for i in range(16)]
    rows += [gg_c[:, 128 * i : 128 * i + 128] for i in range(8)]
    rows.append(jnp.zeros((4, 128), F32))
    pack_o[552:554] = jnp.concatenate(rows, 0).reshape(2, 16, 128).astype(BF)
    pack_o[554:PARTS] = jnp.zeros((PARTS - 554, 16, 128), BF)

    copies = [
        pltpu.make_async_copy(pack_o.at[pl.ds(start, HALF)], o, sems.at[n])
        for n, (o, start) in enumerate(
            ((keep_o, core[0] * HALF), (give_o, (1 - core[0]) * HALF))
        )
    ]
    for x in copies:
        x.start()
    for x in copies:
        x.wait()


def merge_weight_share(core, *refs):
    total = tn(refs[0][...], refs[4][...])
    for k in range(1, 4):
        total = total + tn(refs[k][...], refs[4 + k][...])
    keep_o, give_o = refs[8], refs[9]

    def halves(first, second):
        first[0:64, :] = total[0:64].astype(BF)
        second[0:64, :] = total[64:128].astype(BF)
        first[64:128, :] = total[128:192].astype(BF)
        second[64:128, :] = total[192:256].astype(BF)

    @pl.when(core[0] == 0)
    def _():
        halves(keep_o, give_o)

    @pl.when(core[0] != 0)
    def _():
        halves(give_o, keep_o)


def pack_sums(at, g0, r0, g2, r2, keep, got, out):
    for a, (g, r) in ((at[0], (g0, r0)), (1 - at[0], (g2, r2))):
        head = (g[...].astype(F32) + r[...].astype(F32)).astype(BF)
        for j in range(8):
            row = pl.multiple_of(a * 3200 + 400 * j, 16)
            out[pl.ds(row, 272), :] = head[:, 128 * j : 128 * j + 128]
    merge = keep[...].astype(F32) + got[...].astype(F32)
    for q in range(16):
        rows = merge[8 * q : 8 * q + 8]
        for t in range(8):
            pair = [rows[:, 256 * t : 256 * t + 128], rows[:, 256 * t + 128 : 256 * t + 256]]
            row = 400 * q + 272 + 16 * t
            out[row : row + 16, :] = jnp.concatenate(pair, 0).astype(BF)


def unpack_sums(parts, strip_o, merge_o):
    total = parts[0:400, :].astype(F32)
    for q in range(1, 16):
        total = total + parts[400 * q : 400 * q + 400, :].astype(F32)
    strip_o[...] = total[0:272].astype(BF)
    for t in range(16):
        merge_o[:, 128 * t : 128 * t + 128] = total[272 + 8 * t : 280 + 8 * t]


def coarse_join(at, *refs):
    parts, (gw_o, go_o, gb_o, table) = refs[:4], refs[4:]
    for k in range(4):
        for n in range(2):
            lon = (at[0] + k) % 4 * 2 + (at[1] + n) % 2
            lanes = pl.ds(pl.multiple_of(lon * 128, 128), 128)
            rows = parts[k][272 * n : 272 * n + 272, :].astype(F32)
            gw_o[:, lanes] = rows[0:192]
            go_o[:, lanes] = rows[192:256]
            table[:, lanes] = rows[256:272]
    for t in range(5):
        n = min(16, CELLS - 16 * t)
        gb_o[0, 16 * t : 16 * t + n, :] = table[0:n, 128 * t : 128 * t + CELLS]


def fine_place(win, b, l, d, unroll, out):
    src = jnp.concatenate([win[...], b[...], l[...], d[...]], 0)
    out[...] = nn(unroll[...], src).astype(BF)


def add_two(a, b, out):
    out[...] = (a[...].astype(F32) + b[...].astype(F32)).astype(BF)


def sum_and_copy(parts, out):
    total = parts[0].astype(F32)
    for k in range(1, 64):
        total = total + parts[k].astype(F32)
    total = total.astype(BF)
    for k in range(64):
        out[k] = total


def unpack(core, mine, other, gq_o, gb_o, go_o, gf_o, gm_o, gc_o, pack):
    @pl.when(core[0] == 0)
    def _():
        pack[0:HALF] = mine[...]
        pack[HALF:PARTS] = other[...]

    @pl.when(core[0] != 0)
    def _():
        pack[0:HALF] = other[...]
        pack[HALF:PARTS] = mine[...]

    for i in range(12):
        gq_o[:, 128 * i : 128 * i + 128] = (
            pack[32 * i : 32 * i + 32].astype(F32).reshape(512, 128)
        )
    for i in range(4):
        go_o[:, 128 * i : 128 * i + 128] = (
            pack[384 + 32 * i : 416 + 32 * i].astype(F32).reshape(512, 128)
        )
    for h in range(8):
        t = pack[512 + 5 * h : 517 + 5 * h].astype(F32).reshape(80, 128)
        gb_o[h] = t[:, 0:PAD].T[0:CELLS, 0:CELLS]
    rows = pack[552:554].astype(F32).reshape(32, 128)
    first = 0
    for o, n in ((gf_o, 4), (gm_o, 16), (gc_o, 8)):
        for i in range(n):
            o[:, 128 * i : 128 * i + 128] = rows[first + i : first + i + 1]
        first += n


def count_of(axes):
    n = 1
    for a in axes:
        n *= lax.axis_size(a)
    return n


def shift(x, axes, by):
    n = count_of(axes)
    return lax.ppermute(x, axes, [(i, (i + by) % n) for i in range(n)])


def shift_both(x, by):
    nl, nn_ = count_of(LAT), count_of(LON)
    pairs = [
        (i * nn_ + j, ((i + by) % nl) * nn_ + (j + by) % nn_)
        for i in range(nl)
        for j in range(nn_)
    ]
    return lax.ppermute(x, ALL, pairs)


def exchange(pieces, by):
    lat_piece, lon_piece, corner = pieces
    return shift(lat_piece, LAT, by), shift(lon_piece, LON, by), shift_both(corner, by)


def along_y(x):
    return [x] + [shift(x, ("y",), -k) for k in (1, 2, 3)]


def back_along_y(parts):
    return [parts[0]] + [shift(parts[k], ("y",), k) for k in (1, 2, 3)]


def after(x, *others):
    return lax.optimization_barrier((x, others))[0]


def local(
    fields,
    region_fine,
    region_coarse,
    gain_fine,
    qkv_fine,
    bias_fine,
    out_fine,
    gain_merge,
    merge_weight,
    gain_coarse,
    qkv_coarse,
    bias_coarse,
    out_coarse,
    grad_skip,
    grad_out,
):
    c_roll, c_send, c_unroll = make_fine_roll(), make_fine_send(), make_fine_unroll()
    roll_own, roll_far = make_coarse_roll()
    back_own, back_far = make_coarse_unroll()
    roll_f, send_f, unroll_f = const(c_roll), const(c_send), const(c_unroll)
    order_f = const(c_unroll[patch_order()])
    spread = np.zeros((288, 288), np.float32)
    spread[patch_order(), np.arange(288)] = 1
    spread_f = const(spread)
    send_c, back_c = const(make_coarse_send()), const(make_coarse_back())
    roll_own, roll_far = const(roll_own), const(roll_far)
    back_own, back_far = const(back_own), const(back_far)
    gain_f2, gain_m2, gain_c2 = gain_fine[None], gain_merge[None], gain_coarse[None]

    core = lax.axis_index("c").astype(jnp.int32).reshape(1)
    tile = fields.reshape(288, 512)
    piece = ((32, 1024), BF)
    win = ((320, 512), BF)
    window = ((PAD, 1024), BF)

    *first, go_tile = call(
        first_pieces,
        [((144, 512), BF), ((160, 512), BF), ((96, 512), BF), ((72, 1024), BF)],
        tile, grad_out, send_c,
        late="all",
    )
    first_far = exchange(first, -1)

    (w0,) = call(pack_weights, [((272, 1024), BF)], qkv_coarse.T, out_coarse, bias_coarse)
    w2 = shift(w0, ("xh",), 1)
    w1 = shift(w0, ("c",), 1)

    label_c = jnp.pad(
        region_coarse.reshape(1, 72).astype(F32), ((0, 0), (0, 952)), constant_values=-1.0
    )
    label_f = region_fine.reshape(2, 6, 2, 12).transpose(0, 2, 1, 3).reshape(4, 72).astype(F32)
    label_f = jnp.pad(label_f, ((0, 0), (0, 8)), constant_values=-1.0)

    (gw_win,) = call(
        coarse_window_labelled, [window], go_tile, *first_far, roll_own, roll_far, label_c
    )
    g_all = along_y(gw_win)
    xr, xn, qkv, prob, ctx, skip_win, *skip_pieces = call(
        fine_forward,
        [win, win, ((320, 1536), BF), ((32, PAD, PAD), BF), win, win,
         ((64, 512), BF), ((64, 512), BF), ((32, 512), BF)],
        after(tile, gw_win), *first_far, roll_f, gain_f2, qkv_fine, out_fine, bias_fine, label_f, send_f,
        late="all",
        scratch=[pltpu.VMEM((8, PAD, 128), F32)],
        flops=3_000_000_000,
    )
    s_far = exchange(skip_pieces, 1)
    skip_win = after(skip_win, g_all)
    skip_level, pat, mn, z, zn, *z_pieces = call(
        merge_forward,
        [((288, 512), BF), ((72, 2048), BF), ((72, 2048), BF), ((72, 1024), BF), ((72, 1024), BF),
         piece, piece, piece],
        skip_win, *s_far, unroll_f, order_f, gain_m2, merge_weight, gain_c2, send_c,
        late="all",
        flops=2_500_000_000,
    )
    z_far = exchange(z_pieces, -1)
    (u_win,) = call(coarse_window, [window], zn, *z_far, roll_own, roll_far)
    w3 = shift(after(w2, u_win), ("c",), 1)
    u_all = along_y(u_win)
    mn_own = after(mn, u_all)
    mn_all = [mn_own] + [shift(mn_own, ("y",), k) for k in (1, 2, 3)]
    outs = call(
        coarse_attention,
        [window] * 8 + [((272, 1024), BF)] * 4,
        *u_all, *g_all, w0, w1, w2, w3,
        late="all",
        scratch=[
            pltpu.VMEM((4, 320, 192), BF), pltpu.VMEM((320, 256), BF),
            pltpu.VMEM((4, 320, 192), BF), pltpu.VMEM((4, PAD, 128), F32),
        ],
        flops=9_000_000_000,
    )
    outs = after(outs, mn_all)
    gw0, gw1, gw2, gw3 = outs[8:]
    du_parts = back_along_y(outs[0:4])
    r0 = shift(gw1, ("c",), 1)
    r2 = shift(gw3, ("c",), 1)
    du_parts[0] = after(du_parts[0], r0, r2)
    du_win, *du_pieces = call(coarse_sum, [window] + [piece] * 3, *du_parts, back_c)
    du_far = exchange(du_pieces, 1)
    at_y = lax.axis_index("y").astype(jnp.int32).reshape(1)
    dskip, k_lat, k_lon, k_corner, gg_m, gg_c, *dz_parts = call(
        merge_backward,
        [((288, 512), BF), ((80, 512), BF), ((96, 512), BF), ((32, 512), BF),
         ((1, 2048), F32), ((1, 1024), F32)] + [((72, 256), BF)] * 4,
        at_y, z, go_tile, du_win, *du_far, back_own, back_far, gain_c2, pat, gain_m2, merge_weight,
        grad_skip.reshape(288, 512), spread_f,
        scratch=[pltpu.VMEM((72, 1024), BF)],
        scalars=1,
        late="all",
        flops=3_000_000_000,
    )
    k_far = exchange((k_lat, k_lon, k_corner), -1)
    dz_all = dz_parts[0:1] + [shift(dz_parts[k], ("y",), k) for k in (1, 2, 3)]
    merge_keep, merge_give = call(
        merge_weight_share, [((128, 2048), BF)] * 2, core, *dz_all, *mn_all, scalars=1, late="all"
    )
    merge_got = shift(merge_give, ("c",), 1)
    xh = lax.axis_index("xh").astype(jnp.int32).reshape(1)
    (packed,) = call(
        pack_sums, [((6400, 128), BF)], xh, gw0, r0, gw2, r2, merge_keep, merge_got, scalars=1
    )
    packed = after(packed, k_far)
    sums = lax.all_to_all(packed, ("xh",) + LON, 0, 0, tiled=True)
    dskip = after(dskip, packed)
    dx_win, d_lat, d_lon, d_corner, keep, give = call(
        fine_backward,
        [win, ((64, 512), BF), ((64, 512), BF), ((32, 512), BF),
         ((HALF, 16, 128), BF), ((HALF, 16, 128), BF)],
        core, dskip, *k_far, roll_f, gain_f2, qkv_fine, out_fine, xr, xn, qkv, prob, ctx, send_f,
        gg_m, gg_c,
        late="all",
        scratch=[
            pltpu.VMEM((320, 1536), BF), pltpu.VMEM((8, PAD, 128), F32),
            pltpu.VMEM((PARTS, 16, 128), BF), pltpu.SemaphoreType.DMA((2,)),
        ],
        scalars=1,
        hbm_outs=(4, 5),
        flops=1_000_000,
    )


    strip, merge_t = call(unpack_sums, [((272, 128), BF), ((8, 2048), F32)], sums)
    at_lon = jnp.stack([lax.axis_index("z"), lax.axis_index("xl")]).astype(jnp.int32)

    s_parts = back_along_y([after(x, dx_win) for x in outs[4:8]])
    keep = after(keep, sums, s_parts)
    s_win, s_lat, s_lon, s_corner = call(coarse_sum, [window] + [piece] * 3, *s_parts, back_c)
    (half,) = call(add_two, [((HALF, 16, 128), BF)], keep, shift(give, ("c",), 1), late="all")
    half = after(half, s_corner, strip)
    by_chip = (count_of(CHIPS), HALF * 16 // count_of(CHIPS), 128)
    spread_out = lax.all_to_all(half.reshape(by_chip), CHIPS, 0, 0, tiled=True)
    d_far = exchange((d_lat, d_lon, d_corner), 1)
    s_corner = shift_both(s_corner, 1)
    strips = jnp.concatenate([strip, shift(strip, ("xl",), 1)], 0)
    (copies,) = call(sum_and_copy, [(by_chip, BF)], spread_out)
    copies = after(copies, d_far, s_corner, strips)
    whole_half = lax.all_to_all(copies, CHIPS, 0, 0, tiled=True).reshape(HALF, 16, 128)
    strips, s_lat, s_lon = after((strips, s_lat, s_lon), copies)
    strips = [strips] + [shift(strips, ("z",), -k) for k in (1, 2, 3)]
    s_back = (shift(s_lat, LAT, 1), shift(s_lon, LON, 1), s_corner)
    (output,) = call(
        coarse_output, [((6, 12, 1024), BF)], z, s_win, *s_back, back_own, back_far
    )
    (grad_fields,) = call(fine_place, [((288, 512), BF)], dx_win, *d_far, unroll_f)
    gw_c, go_c, gb_c = call(
        coarse_join, [((192, 1024), F32), ((64, 1024), F32), ((1, CELLS, CELLS), F32)],
        at_lon, *strips,
        scratch=[pltpu.VMEM((16, 1024), F32)], scalars=1,
    )
    whole_half = after(whole_half, merge_t, gw_c, output, grad_fields)
    other_half = shift(whole_half, ("c",), 1)

    gq, gb, go, gg_f, gg_m, gg_c = call(
        unpack,
        [((512, 1536), F32), ((8, CELLS, CELLS), F32), ((512, 512), F32),
         ((1, 512), F32), ((1, 2048), F32), ((1, 1024), F32)],
        core, whole_half, other_half,
        scratch=[pltpu.VMEM((PARTS, 16, 128), BF)],
        scalars=1,
    )
    return (
        skip_level.reshape(12, 24, 512),
        output,
        grad_fields.reshape(12, 24, 512),
        gg_f[0],
        gq,
        gb,
        go,
        gg_m[0],
        merge_t.T,
        gg_c[0],
        gw_c.T,
        gb_c,
        go_c,
    )


def solution(mesh):
    fine_mesh = Mesh(mesh.devices.reshape(4, 2, 2, 4, 2), ALL)
    grid = P(LAT, LON, None)
    placed = (
        grid,
        P(LAT, LON),
        P(LAT, LON),
        P(),
        P(),
        P(),
        P(),
        P(),
        P(),
        P(),
        P(None, LAT),
        P(LAT, None, None),
        P(LAT, None),
        grid,
        grid,
    )
    return jax.shard_map(
        local,
        mesh=fine_mesh,
        in_specs=placed,
        out_specs=(
            grid,
            grid,
            grid,
            P(),
            P(),
            P(),
            P(),
            P(),
            P(None, ALL),
            P(),
            P(None, LAT),
            P(LAT, None, None),
            P(LAT, None),
        ),
        check_vma=False,
    )
```

```python
import jax
import jax.numpy as jnp
import numpy as np
from jax import lax
from jax.experimental import pallas as pl
from jax.experimental.pallas import tpu as pltpu
from jax.sharding import Mesh
from jax.sharding import PartitionSpec as P

EPSILON = 1e-05
MASKED = -1000000000.0
BF = jnp.bfloat16
F32 = jnp.float32
CELLS = 72
PAD = 80
SCALE = 0.125

LAT = ("y", "xh", "c")
LON = ("z", "xl")
ALL = LAT + LON
CHIPS = ("y", "xh", "z", "xl")
HALF = 288
PARTS = 576


def fine_window_row(rr, cc):
    return (rr // 6 * 2 + cc // 12) * PAD + (rr % 6) * 12 + cc % 12


def make_fine_roll():
    m = np.zeros((320, 496), np.float32)
    for rr in range(12):
        for cc in range(24):
            if rr < 9 and cc < 18:
                s = (rr + 3) * 24 + cc + 6
            elif cc < 18:
                s = 288 + (rr - 9) * 24 + cc + 6
            elif rr < 9:
                s = 368 + (rr + 3) * 8 + cc - 18
            else:
                s = 464 + (rr - 9) * 8 + cc - 18
            m[fine_window_row(rr, cc), s] = 1
    return m


def make_fine_send():
    m = np.zeros((160, 320), np.float32)
    for r in range(3):
        for cc in range(18):
            m[r * 18 + cc, fine_window_row(9 + r, cc)] = 1
    for rr in range(9):
        for q in range(6):
            m[64 + rr * 6 + q, fine_window_row(rr, 18 + q)] = 1
    for r in range(3):
        for q in range(6):
            m[128 + r * 6 + q, fine_window_row(9 + r, 18 + q)] = 1
    return m


def make_fine_unroll():
    m = np.zeros((288, 480), np.float32)
    for r in range(12):
        for c in range(24):
            if r >= 3 and c >= 6:
                s = fine_window_row(r - 3, c - 6)
            elif c >= 6:
                s = 320 + r * 18 + c - 6
            elif r >= 3:
                s = 384 + (r - 3) * 6 + c
            else:
                s = 448 + r * 6 + c
            m[r * 24 + c, s] = 1
    return m


def patch_order():
    order = []
    for ro in range(2):
        for co in range(2):
            for r in range(6):
                for c in range(12):
                    order.append((2 * r + ro) * 24 + 2 * c + co)
    return np.array(order)


def make_coarse_send():
    m = np.zeros((96, 72), np.float32)
    for r in range(3):
        for c in range(6):
            m[r * 6 + c, r * 12 + c + 6] = 1
            m[32 + r * 6 + c, (r + 3) * 12 + c] = 1
            m[64 + r * 6 + c, r * 12 + c] = 1
    return m


def make_coarse_roll():
    own = np.zeros((PAD, 72), np.float32)
    far = np.zeros((PAD, 96), np.float32)
    for a in range(6):
        for b in range(12):
            row = a * 12 + b
            if a < 3 and b < 6:
                own[row, (a + 3) * 12 + b + 6] = 1
            elif b < 6:
                far[row, (a - 3) * 6 + b] = 1
            elif a < 3:
                far[row, 32 + a * 6 + b - 6] = 1
            else:
                far[row, 64 + (a - 3) * 6 + b - 6] = 1
    return own, far


def make_coarse_back():
    m = np.zeros((96, PAD), np.float32)
    for r in range(3):
        for c in range(6):
            m[r * 6 + c, (r + 3) * 12 + c] = 1
            m[32 + r * 6 + c, r * 12 + c + 6] = 1
            m[64 + r * 6 + c, (r + 3) * 12 + c + 6] = 1
    return m


def make_coarse_unroll():
    own = np.zeros((72, PAD), np.float32)
    far = np.zeros((72, 96), np.float32)
    for r in range(6):
        for c in range(12):
            row = r * 12 + c
            if r >= 3 and c >= 6:
                own[row, (r - 3) * 12 + c - 6] = 1
            elif c >= 6:
                far[row, r * 6 + c - 6] = 1
            elif r >= 3:
                far[row, 32 + (r - 3) * 6 + c] = 1
            else:
                far[row, 64 + r * 6 + c] = 1
    return own, far


def const(m):
    return jnp.asarray(np.asarray(m, np.float32), BF)


def nn(a, b):
    return lax.dot_general(a, b, (((1,), (0,)), ((), ())), preferred_element_type=F32)


def nt(a, b):
    return lax.dot_general(a, b, (((1,), (1,)), ((), ())), preferred_element_type=F32)


def tn(a, b):
    return lax.dot_general(a, b, (((0,), (0,)), ((), ())), preferred_element_type=F32)


def normalise(x):
    average = jnp.mean(x, -1, keepdims=True)
    centred = x - average
    rstd = lax.rsqrt(jnp.mean(centred * centred, -1, keepdims=True) + EPSILON)
    return centred * rstd, rstd


def norm_back(dy, gain, xhat, rstd):
    dxhat = dy * gain
    m1 = jnp.mean(dxhat, -1, keepdims=True)
    m2 = jnp.mean(dxhat * xhat, -1, keepdims=True)
    return rstd * (dxhat - m1 - xhat * m2)


def allowed_cells(label_row):
    across = jnp.broadcast_to(label_row, (PAD, PAD))
    return across.T == across


def probabilities(q, k, bias_t, allowed):
    scores = nt(k, q) * SCALE + bias_t
    scores = jnp.where(allowed, scores, MASKED)
    weights = jnp.exp(scores - jnp.max(scores, 0, keepdims=True))
    return weights * (1.0 / jnp.sum(weights, 0, keepdims=True))


def score_grad(p, v, dc):
    dp = nt(v, dc)
    inner = jnp.sum(dp * p, 0, keepdims=True)
    return p * (dp - inner)


class Late:
    def __init__(self, copy, ref):
        self.copy, self.ref = copy, ref

    def __getitem__(self, index):
        if self.copy is not None:
            self.copy.wait()
            self.copy = None
        return self.ref[index]

    @property
    def shape(self):
        return self.ref.shape


class Early:
    def __init__(self, copy, ref):
        self.copy, self.ref, self.started = copy, ref, False

    def __getitem__(self, index):
        return self.ref[index]

    def __setitem__(self, index, value):
        self.ref[index] = value

    def flush(self):
        if not self.started:
            self.copy.start()
            self.started = True


def call(body, outs, *args, scratch=(), flops=200_000_000, scalars=0, late=(), mib=None, hbm_outs=(), early=()):
    late = tuple(range(scalars, len(args))) if late == "all" else late
    shapes = [jax.ShapeDtypeStruct(s, d) for s, d in outs]
    spaces = [pltpu.SMEM] * scalars + [pltpu.VMEM] * (len(args) - scalars)
    for i in late:
        spaces[i] = pl.ANY
    buffers = [pltpu.VMEM(args[i].shape, args[i].dtype) for i in late]
    buffers += [pltpu.VMEM(*outs[i]) for i in early]
    if buffers:
        buffers.append(pltpu.SemaphoreType.DMA((len(late) + len(early),)))

    def kernel(*refs):
        refs, spare = refs[: len(refs) - len(buffers)], refs[len(refs) - len(buffers) :]
        refs = list(refs)
        lates = []
        for n, i in enumerate(late):
            copy = pltpu.make_async_copy(refs[i], spare[n], spare[-1].at[n])
            copy.start()
            refs[i] = Late(copy, spare[n])
            lates.append(refs[i])
        earlies = []
        for n, i in enumerate(early, len(late)):
            copy = pltpu.make_async_copy(spare[n], refs[len(args) + i], spare[-1].at[n])
            refs[len(args) + i] = Early(copy, spare[n])
            earlies.append(refs[len(args) + i])
        body(*refs)
        for x in lates:
            assert x.copy is None
        for x in earlies:
            x.flush()
        for x in earlies:
            x.copy.wait()

    return pl.pallas_call(
        kernel,
        out_shape=shapes,
        out_specs=[
            pl.BlockSpec(memory_space=pl.ANY if n in hbm_outs or n in early else pltpu.VMEM)
            for n in range(len(outs))
        ],
        in_specs=[pl.BlockSpec(memory_space=m) for m in spaces],
        scratch_shapes=list(scratch) + buffers,
        compiler_params=pltpu.CompilerParams(vmem_limit_bytes=(mib or (56 if late else 16)) * 1024 * 1024),
        cost_estimate=pl.CostEstimate(flops=flops, bytes_accessed=1_000_000, transcendentals=0),
    )(*args)


def fine_forward(
    f, hl, hn, hd, roll, gain, wqkv, wo, bias, lab, send,
    xr_o, xn_o, qkv_o, p_o, c_o, skip_o, b_o, l_o, d_o,
    table,
):
    src = jnp.concatenate([f[...], hl[0:80, :], hn[0:96, :], hd[0:32, :]], 0)
    xr = nn(roll[...], src)
    xr_o[...] = xr.astype(BF)
    xr_o.flush()
    xhat, _ = normalise(xr)
    xn = (xhat * gain[...]).astype(BF)
    xn_o[...] = xn
    xn_o.flush()
    qkv_o[...] = nn(xn, wqkv[...]).astype(BF)
    qkv_o.flush()
    table[...] = jnp.zeros((8, PAD, 128), F32)
    for h in range(8):
        table[h, 0:CELLS, 0:CELLS] = bias[h].astype(F32)
    biases = [table[h, :, 0:PAD].T for h in range(8)]
    for w in range(4):
        allowed = allowed_cells(lab[w : w + 1, :])
        rows = slice(w * PAD, (w + 1) * PAD)
        for h in range(8):
            at = 192 * h
            q = qkv_o[rows, at : at + 64]
            k = qkv_o[rows, at + 64 : at + 128]
            v = qkv_o[rows, at + 128 : at + 192]
            p = probabilities(q, k, biases[h], allowed).astype(BF)
            p_o[w * 8 + h] = p
            c_o[rows, 64 * h : 64 * h + 64] = tn(p, v).astype(BF)
    p_o.flush()
    c_o.flush()
    skip = (xr + nn(c_o[...], wo[...])).astype(BF)
    skip_o[...] = skip
    pieces = nn(send[...], skip).astype(BF)
    b_o[...] = pieces[:64]
    l_o[...] = pieces[64:128]
    d_o[...] = pieces[128:]


def merge_forward(
    win, b, l, d, unroll, order, gain_m, wm, gain_c, send,
    skip_o, pat_o, mn_o, z_o, zn_o, b_o, l_o, d_o,
):
    src = jnp.concatenate([win[...], b[...], l[...], d[...]], 0)
    skip_o[...] = nn(unroll[...], src).astype(BF)
    cells = nn(order[...], src)
    patches = jnp.concatenate([cells[72 * k : 72 * k + 72] for k in range(4)], 1)
    pat_o[...] = patches.astype(BF)
    mhat, _ = normalise(patches)
    mn = (mhat * gain_m[...]).astype(BF)
    mn_o[...] = mn
    z = nn(mn, wm[...]).astype(BF)
    z_o[...] = z
    zhat, _ = normalise(z.astype(F32))
    zn = (zhat * gain_c[...]).astype(BF)
    zn_o[...] = zn
    pieces = nn(send[...], zn).astype(BF)
    b_o[...] = pieces[0:32]
    l_o[...] = pieces[32:64]
    d_o[...] = pieces[64:96]


def first_pieces(f, go, send, lat_o, lon_o, corner_o, tile_o):
    tile = jnp.concatenate([go[r].astype(F32) for r in range(6)], 0).astype(BF)
    tile_o[...] = tile
    pieces = nn(send[...], tile).astype(BF)
    fine = f[...]
    cells = fine.astype(F32).reshape(12, 24, 512)
    lat_o[0:80, :] = fine[0:80]
    lon_o[0:96, :] = cells[:, 0:8].reshape(96, 512).astype(BF)
    corner_o[0:32, :] = cells[0:4, 0:8].reshape(32, 512).astype(BF)
    for i, (o, at) in enumerate(((lat_o, 80), (lon_o, 96), (corner_o, 32))):
        o[at : at + 32, :] = pieces[32 * i : 32 * i + 32, 0:512]
        o[at + 32 : at + 64, :] = pieces[32 * i : 32 * i + 32, 512:]


def pack_weights(w, o, bias, out):
    out[0:192, :] = w[...]
    out[192:256, :] = o[...]
    out[256:272, :] = jnp.zeros((16, 1024), BF)
    for t in range(5):
        n = min(16, CELLS - 16 * t)
        rows = bias[0, 16 * t : 16 * t + n, :]
        out[256 : 256 + n, 128 * t : 128 * t + CELLS] = rows


def coarse_window(tile, b, l, d, own, far, out):
    src = jnp.concatenate([b[...], l[...], d[...]], 0)
    out[...] = (nn(own[...], tile[...]) + nn(far[...], src)).astype(BF)


def coarse_window_labelled(tile, b, l, d, own, far, lab, out):
    parts = []
    for r, at in ((b, 80), (l, 96), (d, 32)):
        parts.append(jnp.concatenate([r[at : at + 32, :], r[at + 32 : at + 64, :]], 1))
    rows = nn(own[...], tile[...]) + nn(far[...], jnp.concatenate(parts, 0))
    at = lax.broadcasted_iota(jnp.int32, rows.shape, 0)
    out[...] = jnp.where(at == CELLS, jnp.broadcast_to(lab[...], rows.shape), rows).astype(BF)


def coarse_attention(
    u0, u1, u2, u3, g0, g1, g2, g3, w0, w1, w2, w3,
    d0, d1, d2, d3, s0, s1, s2, s3, gw0, gw1, gw2, gw3,
    qkv, ctx, dqkv, bias_sum,
):
    ws = (w0, w1, w2, w3)
    u = jnp.concatenate([r[...] for r in (u0, u1, u2, u3)], 0)
    live = lax.broadcasted_iota(jnp.int32, (PAD, 1024), 0) < CELLS
    labels = []
    parts = []
    for r in (g0, g1, g2, g3):
        rows = r[...].astype(F32)
        labels.append(rows[CELLS : CELLS + 1, 0:PAD])
        parts.append(jnp.where(live, rows, 0.0).astype(BF))
    g = jnp.concatenate(parts, 0)
    wo = jnp.concatenate([r[192:256, :] for r in ws], 0)
    dc = nt(g, wo).astype(BF)
    for s in range(4):
        qkv[s] = nt(u, ws[s][0:192, :]).astype(BF)
    masks = [allowed_cells(row) for row in labels]
    for s in range(4):
        groups = [ws[s][256:272, 128 * t : 128 * t + PAD] for t in range(5)]
        bias = jnp.concatenate(groups, 0).astype(F32).T
        total = jnp.zeros((PAD, PAD), F32)
        for w in range(4):
            rows = slice(w * PAD, (w + 1) * PAD)
            q = qkv[s, rows, 0:64]
            k = qkv[s, rows, 64:128]
            v = qkv[s, rows, 128:192]
            p = probabilities(q, k, bias, masks[w])
            pb = p.astype(BF)
            ctx[rows, 64 * s : 64 * s + 64] = tn(pb, v).astype(BF)
            dch = dc[rows, 64 * s : 64 * s + 64]
            ds = score_grad(p, v, dch)
            total = total + ds
            dsb = ds.astype(BF)
            dqkv[s, rows, 0:64] = (tn(dsb, k) * SCALE).astype(BF)
            dqkv[s, rows, 64:128] = (nn(dsb, q) * SCALE).astype(BF)
            dqkv[s, rows, 128:192] = nn(pb, dch).astype(BF)
        bias_sum[s, :, 0:PAD] = total.T
    bias_sum[:, :, PAD:] = jnp.zeros((4, PAD, 128 - PAD), F32)
    c = ctx[...]
    out = nn(c, wo)
    du = nn(dqkv[0], w0[0:192, :])
    for s in range(1, 4):
        du = du + nn(dqkv[s], ws[s][0:192, :])
    for w, (do, so) in enumerate(((d0, s0), (d1, s1), (d2, s2), (d3, s3))):
        do[...] = du[w * PAD : (w + 1) * PAD].astype(BF)
        so[...] = out[w * PAD : (w + 1) * PAD].astype(BF)
    gwo = tn(c, g).astype(BF)
    for s, o in enumerate((gw0, gw1, gw2, gw3)):
        o[0:192, :] = tn(dqkv[s], u).astype(BF)
        o[192:256, :] = gwo[64 * s : 64 * s + 64]
        o[256:272, 640:] = jnp.zeros((16, 384), BF)
        for t in range(5):
            o[256:272, 128 * t : 128 * t + 128] = bias_sum[s, 16 * t : 16 * t + 16].astype(BF)


def coarse_sum(a0, a1, a2, a3, back, own_o, b_o, l_o, d_o):
    total = a0[...].astype(F32) + a1[...].astype(F32) + a2[...].astype(F32) + a3[...].astype(F32)
    total = total.astype(BF)
    own_o[...] = total
    pieces = nn(back[...], total).astype(BF)
    b_o[...] = pieces[0:32]
    l_o[...] = pieces[32:64]
    d_o[...] = pieces[64:96]


def coarse_output(z, own, b, l, d, uown, ufar, out_o):
    far = jnp.concatenate([b[...], l[...], d[...]], 0)
    s = nn(uown[...], own[...]) + nn(ufar[...], far)
    rows = z[...].astype(F32) + s
    for r in range(6):
        out_o[r] = rows[12 * r : 12 * r + 12].astype(BF)


def merge_backward(
    at, z, go, own, b, l, d, uown, ufar, gain_c, pat, gain_m, wm, gskip, spread,
    dskip_o, top_o, side_o, corner_o, gg_m, gg_c, *dz_os,
):
    far = jnp.concatenate([b[...], l[...], d[...]], 0)
    dzn = nn(uown[...], own[...]) + nn(ufar[...], far)
    z32 = z[...].astype(F32)
    zhat, rstd = normalise(z32)
    gg_c[...] = jnp.sum(dzn * zhat, 0, keepdims=True)
    dz = (go[...].astype(F32) + norm_back(dzn, gain_c[...], zhat, rstd)).astype(BF)
    table = dz_os[4]
    table[...] = dz
    for k in range(4):
        dz_os[k][...] = table[:, pl.ds(pl.multiple_of((at[0] + k) % 4 * 256, 256), 256)]
    dmn = nt(dz, wm[...])
    mhat, mrstd = normalise(pat[...].astype(F32))
    gg_m[...] = jnp.sum(dmn * mhat, 0, keepdims=True)
    dpat = norm_back(dmn, gain_m[...], mhat, mrstd).astype(BF)
    cells = jnp.concatenate([dpat[:, 512 * k : 512 * k + 512] for k in range(4)], 0)
    dskip = (gskip[...].astype(F32) + nn(spread[...], cells)).astype(BF)
    dskip_o[...] = dskip
    top_o[...] = dskip[0:80]
    cells = dskip.astype(F32).reshape(12, 24, 512)
    side_o[...] = cells[:, 0:8].reshape(96, 512).astype(BF)
    corner_o[...] = cells[0:4, 0:8].reshape(32, 512).astype(BF)


def fine_backward(
    core, f, hl, hn, hd, roll, gain, wqkv, wo, xr, xn, qkv, p_in, c, send, gg_m, gg_c,
    dx_o, b_o, l_o, d_o, keep_o, give_o,
    dqkv, bias_sum, pack_o, sems,
):
    src = jnp.concatenate([f[...], hl[...], hn[...], hd[...]], 0)
    g32 = nn(roll[...], src)
    g = g32.astype(BF)
    dc = nt(g, wo[...]).astype(BF)
    bias_sum[...] = jnp.zeros((8, PAD, 128), F32)
    for h in range(8):
        at = 192 * h
        total = jnp.zeros((PAD, PAD), F32)
        for w in range(4):
            rows = slice(w * PAD, (w + 1) * PAD)
            q = qkv[rows, at : at + 64]
            k = qkv[rows, at + 64 : at + 128]
            v = qkv[rows, at + 128 : at + 192]
            pb = p_in[w * 8 + h]
            dch = dc[rows, 64 * h : 64 * h + 64]
            ds = score_grad(pb.astype(F32), v, dch)
            total = total + ds
            dsb = ds.astype(BF)
            dqkv[rows, at : at + 64] = (tn(dsb, k) * SCALE).astype(BF)
            dqkv[rows, at + 64 : at + 128] = (nn(dsb, q) * SCALE).astype(BF)
            dqkv[rows, at + 128 : at + 192] = nn(pb, dch).astype(BF)
        bias_sum[h, :, 0:PAD] = total
    dproj = dqkv[...]
    du = nt(dproj, wqkv[...])
    xhat, rstd = normalise(xr[...].astype(F32))
    gg_f = jnp.sum(du * xhat, 0, keepdims=True)
    dx = (g32 + norm_back(du, gain[...], xhat, rstd)).astype(BF)
    dx_o[...] = dx
    pieces = nn(send[...], dx).astype(BF)
    b_o[...] = pieces[:64]
    l_o[...] = pieces[64:128]
    d_o[...] = pieces[128:]
    gq = tn(xn[...], dproj)
    for i in range(12):
        pack_o[32 * i : 32 * i + 32] = gq[:, 128 * i : 128 * i + 128].reshape(32, 16, 128).astype(BF)
    go = tn(c[...], g)
    for i in range(4):
        pack_o[384 + 32 * i : 416 + 32 * i] = (
            go[:, 128 * i : 128 * i + 128].reshape(32, 16, 128).astype(BF)
        )
    for h in range(8):
        pack_o[512 + 5 * h : 517 + 5 * h] = bias_sum[h].reshape(5, 16, 128).astype(BF)
    rows = [gg_f[:, 128 * i : 128 * i + 128] for i in range(4)]
    rows += [gg_m[:, 128 * i : 128 * i + 128] for i in range(16)]
    rows += [gg_c[:, 128 * i : 128 * i + 128] for i in range(8)]
    rows.append(jnp.zeros((4, 128), F32))
    pack_o[552:554] = jnp.concatenate(rows, 0).reshape(2, 16, 128).astype(BF)
    pack_o[554:PARTS] = jnp.zeros((PARTS - 554, 16, 128), BF)

    copies = [
        pltpu.make_async_copy(pack_o.at[pl.ds(start, HALF)], o, sems.at[n])
        for n, (o, start) in enumerate(
            ((keep_o, core[0] * HALF), (give_o, (1 - core[0]) * HALF))
        )
    ]
    for x in copies:
        x.start()
    for x in copies:
        x.wait()


def merge_weight_share(core, *refs):
    total = tn(refs[0][...], refs[4][...])
    for k in range(1, 4):
        total = total + tn(refs[k][...], refs[4 + k][...])
    keep_o, give_o = refs[8], refs[9]

    def halves(first, second):
        first[0:64, :] = total[0:64].astype(BF)
        second[0:64, :] = total[64:128].astype(BF)
        first[64:128, :] = total[128:192].astype(BF)
        second[64:128, :] = total[192:256].astype(BF)

    @pl.when(core[0] == 0)
    def _():
        halves(keep_o, give_o)

    @pl.when(core[0] != 0)
    def _():
        halves(give_o, keep_o)


def pack_sums(at, g0, r0, g2, r2, keep, got, out):
    for a, (g, r) in ((at[0], (g0, r0)), (1 - at[0], (g2, r2))):
        head = (g[...].astype(F32) + r[...].astype(F32)).astype(BF)
        for j in range(8):
            row = pl.multiple_of(a * 3200 + 400 * j, 16)
            out[pl.ds(row, 272), :] = head[:, 128 * j : 128 * j + 128]
    merge = keep[...].astype(F32) + got[...].astype(F32)
    for q in range(16):
        rows = merge[8 * q : 8 * q + 8]
        for t in range(8):
            pair = [rows[:, 256 * t : 256 * t + 128], rows[:, 256 * t + 128 : 256 * t + 256]]
            row = 400 * q + 272 + 16 * t
            out[row : row + 16, :] = jnp.concatenate(pair, 0).astype(BF)


def unpack_sums(parts, strip_o, merge_o):
    total = parts[0:400, :].astype(F32)
    for q in range(1, 16):
        total = total + parts[400 * q : 400 * q + 400, :].astype(F32)
    strip_o[...] = total[0:272].astype(BF)
    for t in range(16):
        merge_o[:, 128 * t : 128 * t + 128] = total[272 + 8 * t : 280 + 8 * t]


def coarse_join(at, *refs):
    parts, (gw_o, go_o, gb_o, table) = refs[:4], refs[4:]
    for k in range(4):
        for n in range(2):
            lon = (at[0] + k) % 4 * 2 + (at[1] + n) % 2
            lanes = pl.ds(pl.multiple_of(lon * 128, 128), 128)
            rows = parts[k][272 * n : 272 * n + 272, :].astype(F32)
            gw_o[:, lanes] = rows[0:192]
            go_o[:, lanes] = rows[192:256]
            table[:, lanes] = rows[256:272]
    for t in range(5):
        n = min(16, CELLS - 16 * t)
        gb_o[0, 16 * t : 16 * t + n, :] = table[0:n, 128 * t : 128 * t + CELLS]


def fine_place(win, b, l, d, unroll, out):
    src = jnp.concatenate([win[...], b[...], l[...], d[...]], 0)
    out[...] = nn(unroll[...], src).astype(BF)


def add_two(a, b, out):
    out[...] = (a[...].astype(F32) + b[...].astype(F32)).astype(BF)


def sum_and_copy(parts, out):
    total = parts[0].astype(F32)
    for k in range(1, 64):
        total = total + parts[k].astype(F32)
    total = total.astype(BF)
    for k in range(64):
        out[k] = total


def unpack(core, mine, other, gq_o, gb_o, go_o, gf_o, gm_o, gc_o, pack):
    @pl.when(core[0] == 0)
    def _():
        pack[0:HALF] = mine[...]
        pack[HALF:PARTS] = other[...]

    @pl.when(core[0] != 0)
    def _():
        pack[0:HALF] = other[...]
        pack[HALF:PARTS] = mine[...]

    for i in range(12):
        gq_o[:, 128 * i : 128 * i + 128] = (
            pack[32 * i : 32 * i + 32].astype(F32).reshape(512, 128)
        )
    for i in range(4):
        go_o[:, 128 * i : 128 * i + 128] = (
            pack[384 + 32 * i : 416 + 32 * i].astype(F32).reshape(512, 128)
        )
    for h in range(8):
        t = pack[512 + 5 * h : 517 + 5 * h].astype(F32).reshape(80, 128)
        gb_o[h] = t[:, 0:PAD].T[0:CELLS, 0:CELLS]
    rows = pack[552:554].astype(F32).reshape(32, 128)
    first = 0
    for o, n in ((gf_o, 4), (gm_o, 16), (gc_o, 8)):
        for i in range(n):
            o[:, 128 * i : 128 * i + 128] = rows[first + i : first + i + 1]
        first += n


def count_of(axes):
    n = 1
    for a in axes:
        n *= lax.axis_size(a)
    return n


def shift(x, axes, by):
    n = count_of(axes)
    return lax.ppermute(x, axes, [(i, (i + by) % n) for i in range(n)])


def shift_both(x, by):
    nl, nn_ = count_of(LAT), count_of(LON)
    pairs = [
        (i * nn_ + j, ((i + by) % nl) * nn_ + (j + by) % nn_)
        for i in range(nl)
        for j in range(nn_)
    ]
    return lax.ppermute(x, ALL, pairs)


def exchange(pieces, by):
    lat_piece, lon_piece, corner = pieces
    return shift(lat_piece, LAT, by), shift(lon_piece, LON, by), shift_both(corner, by)


def along_y(x):
    return [x] + [shift(x, ("y",), -k) for k in (1, 2, 3)]


def back_along_y(parts):
    return [parts[0]] + [shift(parts[k], ("y",), k) for k in (1, 2, 3)]


def after(x, *others):
    return lax.optimization_barrier((x, others))[0]


def local(
    fields,
    region_fine,
    region_coarse,
    gain_fine,
    qkv_fine,
    bias_fine,
    out_fine,
    gain_merge,
    merge_weight,
    gain_coarse,
    qkv_coarse,
    bias_coarse,
    out_coarse,
    grad_skip,
    grad_out,
):
    c_roll, c_send, c_unroll = make_fine_roll(), make_fine_send(), make_fine_unroll()
    roll_own, roll_far = make_coarse_roll()
    back_own, back_far = make_coarse_unroll()
    roll_f, send_f, unroll_f = const(c_roll), const(c_send), const(c_unroll)
    order_f = const(c_unroll[patch_order()])
    spread = np.zeros((288, 288), np.float32)
    spread[patch_order(), np.arange(288)] = 1
    spread_f = const(spread)
    send_c, back_c = const(make_coarse_send()), const(make_coarse_back())
    roll_own, roll_far = const(roll_own), const(roll_far)
    back_own, back_far = const(back_own), const(back_far)
    gain_f2, gain_m2, gain_c2 = gain_fine[None], gain_merge[None], gain_coarse[None]

    core = lax.axis_index("c").astype(jnp.int32).reshape(1)
    tile = fields.reshape(288, 512)
    piece = ((32, 1024), BF)
    win = ((320, 512), BF)
    window = ((PAD, 1024), BF)

    *first, go_tile = call(
        first_pieces,
        [((144, 512), BF), ((160, 512), BF), ((96, 512), BF), ((72, 1024), BF)],
        tile, grad_out, send_c,
        late="all",
    )
    first_far = exchange(first, -1)

    (w0,) = call(pack_weights, [((272, 1024), BF)], qkv_coarse.T, out_coarse, bias_coarse)
    w2 = shift(w0, ("xh",), 1)
    w1 = shift(w0, ("c",), 1)

    label_c = jnp.pad(
        region_coarse.reshape(1, 72).astype(F32), ((0, 0), (0, 952)), constant_values=-1.0
    )
    label_f = region_fine.reshape(2, 6, 2, 12).transpose(0, 2, 1, 3).reshape(4, 72).astype(F32)
    label_f = jnp.pad(label_f, ((0, 0), (0, 8)), constant_values=-1.0)

    (gw_win,) = call(
        coarse_window_labelled, [window], go_tile, *first_far, roll_own, roll_far, label_c
    )
    g_all = along_y(gw_win)
    xr, xn, qkv, prob, ctx, skip_win, *skip_pieces = call(
        fine_forward,
        [win, win, ((320, 1536), BF), ((32, PAD, PAD), BF), win, win,
         ((64, 512), BF), ((64, 512), BF), ((32, 512), BF)],
        after(tile, gw_win), *first_far, roll_f, gain_f2, qkv_fine, out_fine, bias_fine, label_f, send_f,
        late="all",
        scratch=[pltpu.VMEM((8, PAD, 128), F32)],
        early=(0, 1, 2, 3, 4),
        flops=3_000_000_000,
    )
    s_far = exchange(skip_pieces, 1)
    skip_win = after(skip_win, g_all)
    skip_level, pat, mn, z, zn, *z_pieces = call(
        merge_forward,
        [((288, 512), BF), ((72, 2048), BF), ((72, 2048), BF), ((72, 1024), BF), ((72, 1024), BF),
         piece, piece, piece],
        skip_win, *s_far, unroll_f, order_f, gain_m2, merge_weight, gain_c2, send_c,
        late="all",
        flops=2_500_000_000,
    )
    z_far = exchange(z_pieces, -1)
    (u_win,) = call(coarse_window, [window], zn, *z_far, roll_own, roll_far)
    w3 = shift(after(w2, u_win), ("c",), 1)
    u_all = along_y(u_win)
    outs = call(
        coarse_attention,
        [window] * 8 + [((272, 1024), BF)] * 4,
        *u_all, *g_all, w0, w1, w2, w3,
        late="all",
        scratch=[
            pltpu.VMEM((4, 320, 192), BF), pltpu.VMEM((320, 256), BF),
            pltpu.VMEM((4, 320, 192), BF), pltpu.VMEM((4, PAD, 128), F32),
        ],
        flops=9_000_000_000,
    )
    gw0, gw1, gw2, gw3 = outs[8:]
    du_parts = back_along_y(outs[0:4])
    r0 = shift(gw1, ("c",), 1)
    r2 = shift(gw3, ("c",), 1)
    du_parts[0] = after(du_parts[0], r0, r2)
    du_win, *du_pieces = call(coarse_sum, [window] + [piece] * 3, *du_parts, back_c)
    du_far = exchange(du_pieces, 1)
    mn_own = after(mn, du_win)
    mn_all = [mn_own] + [shift(mn_own, ("y",), k) for k in (1, 2, 3)]
    at_y = lax.axis_index("y").astype(jnp.int32).reshape(1)
    dskip, k_lat, k_lon, k_corner, gg_m, gg_c, *dz_parts = call(
        merge_backward,
        [((288, 512), BF), ((80, 512), BF), ((96, 512), BF), ((32, 512), BF),
         ((1, 2048), F32), ((1, 1024), F32)] + [((72, 256), BF)] * 4,
        at_y, z, go_tile, du_win, *du_far, back_own, back_far, gain_c2, pat, gain_m2, merge_weight,
        grad_skip.reshape(288, 512), spread_f,
        scratch=[pltpu.VMEM((72, 1024), BF)],
        scalars=1,
        late="all",
        flops=3_000_000_000,
    )
    k_far = exchange((k_lat, k_lon, k_corner), -1)
    dz_all = dz_parts[0:1] + [shift(dz_parts[k], ("y",), k) for k in (1, 2, 3)]
    merge_keep, merge_give = call(
        merge_weight_share, [((128, 2048), BF)] * 2, core, *dz_all, *mn_all, scalars=1, late="all"
    )
    merge_got = shift(merge_give, ("c",), 1)
    xh = lax.axis_index("xh").astype(jnp.int32).reshape(1)
    (packed,) = call(
        pack_sums, [((6400, 128), BF)], xh, gw0, r0, gw2, r2, merge_keep, merge_got, scalars=1
    )
    packed = after(packed, k_far)
    sums = lax.all_to_all(packed, ("xh",) + LON, 0, 0, tiled=True)
    dskip = after(dskip, packed)
    dx_win, d_lat, d_lon, d_corner, keep, give = call(
        fine_backward,
        [win, ((64, 512), BF), ((64, 512), BF), ((32, 512), BF),
         ((HALF, 16, 128), BF), ((HALF, 16, 128), BF)],
        core, dskip, *k_far, roll_f, gain_f2, qkv_fine, out_fine, xr, xn, qkv, prob, ctx, send_f,
        gg_m, gg_c,
        late="all",
        scratch=[
            pltpu.VMEM((320, 1536), BF), pltpu.VMEM((8, PAD, 128), F32),
            pltpu.VMEM((PARTS, 16, 128), BF), pltpu.SemaphoreType.DMA((2,)),
        ],
        scalars=1,
        hbm_outs=(4, 5),
        flops=1_000_000,
    )


    strip, merge_t = call(unpack_sums, [((272, 128), BF), ((8, 2048), F32)], sums)
    at_lon = jnp.stack([lax.axis_index("z"), lax.axis_index("xl")]).astype(jnp.int32)

    s_parts = back_along_y([after(x, dx_win) for x in outs[4:8]])
    keep = after(keep, sums, s_parts)
    s_win, s_lat, s_lon, s_corner = call(coarse_sum, [window] + [piece] * 3, *s_parts, back_c)
    (half,) = call(add_two, [((HALF, 16, 128), BF)], keep, shift(give, ("c",), 1), late="all")
    half = after(half, s_corner, strip)
    by_chip = (count_of(CHIPS), HALF * 16 // count_of(CHIPS), 128)
    spread_out = lax.all_to_all(half.reshape(by_chip), CHIPS, 0, 0, tiled=True)
    d_far = exchange((d_lat, d_lon, d_corner), 1)
    s_corner = shift_both(s_corner, 1)
    strips = jnp.concatenate([strip, shift(strip, ("xl",), 1)], 0)
    (copies,) = call(sum_and_copy, [(by_chip, BF)], spread_out)
    copies = after(copies, d_far, s_corner, strips)
    whole_half = lax.all_to_all(copies, CHIPS, 0, 0, tiled=True).reshape(HALF, 16, 128)
    strips, s_lat, s_lon = after((strips, s_lat, s_lon), copies)
    strips = [strips] + [shift(strips, ("z",), -k) for k in (1, 2, 3)]
    s_back = (shift(s_lat, LAT, 1), shift(s_lon, LON, 1), s_corner)
    (output,) = call(
        coarse_output, [((6, 12, 1024), BF)], z, s_win, *s_back, back_own, back_far
    )
    (grad_fields,) = call(fine_place, [((288, 512), BF)], dx_win, *d_far, unroll_f)
    gw_c, go_c, gb_c = call(
        coarse_join, [((192, 1024), F32), ((64, 1024), F32), ((1, CELLS, CELLS), F32)],
        at_lon, *strips,
        scratch=[pltpu.VMEM((16, 1024), F32)], scalars=1,
    )
    whole_half = after(whole_half, merge_t, gw_c, output, grad_fields)
    other_half = shift(whole_half, ("c",), 1)

    gq, gb, go, gg_f, gg_m, gg_c = call(
        unpack,
        [((512, 1536), F32), ((8, CELLS, CELLS), F32), ((512, 512), F32),
         ((1, 512), F32), ((1, 2048), F32), ((1, 1024), F32)],
        core, whole_half, other_half,
        scratch=[pltpu.VMEM((PARTS, 16, 128), BF)],
        scalars=1,
    )
    return (
        skip_level.reshape(12, 24, 512),
        output,
        grad_fields.reshape(12, 24, 512),
        gg_f[0],
        gq,
        gb,
        go,
        gg_m[0],
        merge_t.T,
        gg_c[0],
        gw_c.T,
        gb_c,
        go_c,
    )


def solution(mesh):
    fine_mesh = Mesh(mesh.devices.reshape(4, 2, 2, 4, 2), ALL)
    grid = P(LAT, LON, None)
    placed = (
        grid,
        P(LAT, LON),
        P(LAT, LON),
        P(),
        P(),
        P(),
        P(),
        P(),
        P(),
        P(),
        P(None, LAT),
        P(LAT, None, None),
        P(LAT, None),
        grid,
        grid,
    )
    return jax.shard_map(
        local,
        mesh=fine_mesh,
        in_specs=placed,
        out_specs=(
            grid,
            grid,
            grid,
            P(),
            P(),
            P(),
            P(),
            P(),
            P(None, ALL),
            P(),
            P(None, LAT),
            P(LAT, None, None),
            P(LAT, None),
        ),
        check_vma=False,
    )
```

```python
import jax
import jax.numpy as jnp
import numpy as np
from jax import lax
from jax.experimental import pallas as pl
from jax.experimental.pallas import tpu as pltpu
from jax.sharding import Mesh
from jax.sharding import PartitionSpec as P

EPSILON = 1e-05
MASKED = -1000000000.0
BF = jnp.bfloat16
F32 = jnp.float32
CELLS = 72
PAD = 80
SCALE = 0.125

LAT = ("y", "xh", "c")
LON = ("z", "xl")
ALL = LAT + LON
CHIPS = ("y", "xh", "z", "xl")
HALF = 288
PARTS = 576


def fine_window_row(rr, cc):
    return (rr // 6 * 2 + cc // 12) * PAD + (rr % 6) * 12 + cc % 12


def make_fine_roll():
    m = np.zeros((320, 496), np.float32)
    for rr in range(12):
        for cc in range(24):
            if rr < 9 and cc < 18:
                s = (rr + 3) * 24 + cc + 6
            elif cc < 18:
                s = 288 + (rr - 9) * 24 + cc + 6
            elif rr < 9:
                s = 368 + (rr + 3) * 8 + cc - 18
            else:
                s = 464 + (rr - 9) * 8 + cc - 18
            m[fine_window_row(rr, cc), s] = 1
    return m


def make_fine_send():
    m = np.zeros((160, 320), np.float32)
    for r in range(3):
        for cc in range(18):
            m[r * 18 + cc, fine_window_row(9 + r, cc)] = 1
    for rr in range(9):
        for q in range(6):
            m[64 + rr * 6 + q, fine_window_row(rr, 18 + q)] = 1
    for r in range(3):
        for q in range(6):
            m[128 + r * 6 + q, fine_window_row(9 + r, 18 + q)] = 1
    return m


def make_fine_unroll():
    m = np.zeros((288, 480), np.float32)
    for r in range(12):
        for c in range(24):
            if r >= 3 and c >= 6:
                s = fine_window_row(r - 3, c - 6)
            elif c >= 6:
                s = 320 + r * 18 + c - 6
            elif r >= 3:
                s = 384 + (r - 3) * 6 + c
            else:
                s = 448 + r * 6 + c
            m[r * 24 + c, s] = 1
    return m


def patch_order():
    order = []
    for ro in range(2):
        for co in range(2):
            for r in range(6):
                for c in range(12):
                    order.append((2 * r + ro) * 24 + 2 * c + co)
    return np.array(order)


def make_coarse_send():
    m = np.zeros((96, 72), np.float32)
    for r in range(3):
        for c in range(6):
            m[r * 6 + c, r * 12 + c + 6] = 1
            m[32 + r * 6 + c, (r + 3) * 12 + c] = 1
            m[64 + r * 6 + c, r * 12 + c] = 1
    return m


def make_coarse_roll():
    own = np.zeros((PAD, 72), np.float32)
    far = np.zeros((PAD, 96), np.float32)
    for a in range(6):
        for b in range(12):
            row = a * 12 + b
            if a < 3 and b < 6:
                own[row, (a + 3) * 12 + b + 6] = 1
            elif b < 6:
                far[row, (a - 3) * 6 + b] = 1
            elif a < 3:
                far[row, 32 + a * 6 + b - 6] = 1
            else:
                far[row, 64 + (a - 3) * 6 + b - 6] = 1
    return own, far


def make_coarse_back():
    m = np.zeros((96, CELLS), np.float32)
    for r in range(3):
        for c in range(6):
            m[r * 6 + c, (r + 3) * 12 + c] = 1
            m[32 + r * 6 + c, r * 12 + c + 6] = 1
            m[64 + r * 6 + c, (r + 3) * 12 + c + 6] = 1
    return m


def make_coarse_unroll():
    own = np.zeros((72, CELLS), np.float32)
    far = np.zeros((72, 96), np.float32)
    for r in range(6):
        for c in range(12):
            row = r * 12 + c
            if r >= 3 and c >= 6:
                own[row, (r - 3) * 12 + c - 6] = 1
            elif c >= 6:
                far[row, r * 6 + c - 6] = 1
            elif r >= 3:
                far[row, 32 + (r - 3) * 6 + c] = 1
            else:
                far[row, 64 + r * 6 + c] = 1
    return own, far


def const(m):
    return jnp.asarray(np.asarray(m, np.float32), BF)


def nn(a, b):
    return lax.dot_general(a, b, (((1,), (0,)), ((), ())), preferred_element_type=F32)


def nt(a, b):
    return lax.dot_general(a, b, (((1,), (1,)), ((), ())), preferred_element_type=F32)


def tn(a, b):
    return lax.dot_general(a, b, (((0,), (0,)), ((), ())), preferred_element_type=F32)


def normalise(x):
    average = jnp.mean(x, -1, keepdims=True)
    centred = x - average
    rstd = lax.rsqrt(jnp.mean(centred * centred, -1, keepdims=True) + EPSILON)
    return centred * rstd, rstd


def norm_back(dy, gain, xhat, rstd):
    dxhat = dy * gain
    m1 = jnp.mean(dxhat, -1, keepdims=True)
    m2 = jnp.mean(dxhat * xhat, -1, keepdims=True)
    return rstd * (dxhat - m1 - xhat * m2)


def allowed_cells(label_row):
    across = jnp.broadcast_to(label_row, (PAD, PAD))
    return across.T == across


def probabilities(q, k, bias_t, allowed):
    scores = nt(k, q) * SCALE + bias_t
    scores = jnp.where(allowed, scores, MASKED)
    weights = jnp.exp(scores - jnp.max(scores, 0, keepdims=True))
    return weights * (1.0 / jnp.sum(weights, 0, keepdims=True))


def score_grad(p, v, dc):
    dp = nt(v, dc)
    inner = jnp.sum(dp * p, 0, keepdims=True)
    return p * (dp - inner)


class Late:
    def __init__(self, copy, ref):
        self.copy, self.ref = copy, ref

    def __getitem__(self, index):
        if self.copy is not None:
            self.copy.wait()
            self.copy = None
        return self.ref[index]

    @property
    def shape(self):
        return self.ref.shape


class Early:
    def __init__(self, copy, ref):
        self.copy, self.ref, self.started = copy, ref, False

    def __getitem__(self, index):
        return self.ref[index]

    def __setitem__(self, index, value):
        self.ref[index] = value

    def flush(self):
        if not self.started:
            self.copy.start()
            self.started = True


def call(body, outs, *args, scratch=(), flops=200_000_000, scalars=0, late=(), mib=None, hbm_outs=(), early=()):
    late = tuple(range(scalars, len(args))) if late == "all" else late
    shapes = [jax.ShapeDtypeStruct(s, d) for s, d in outs]
    spaces = [pltpu.SMEM] * scalars + [pltpu.VMEM] * (len(args) - scalars)
    for i in late:
        spaces[i] = pl.ANY
    buffers = [pltpu.VMEM(args[i].shape, args[i].dtype) for i in late]
    buffers += [pltpu.VMEM(*outs[i]) for i in early]
    if buffers:
        buffers.append(pltpu.SemaphoreType.DMA((len(late) + len(early),)))

    def kernel(*refs):
        refs, spare = refs[: len(refs) - len(buffers)], refs[len(refs) - len(buffers) :]
        refs = list(refs)
        lates = []
        for n, i in enumerate(late):
            copy = pltpu.make_async_copy(refs[i], spare[n], spare[-1].at[n])
            copy.start()
            refs[i] = Late(copy, spare[n])
            lates.append(refs[i])
        earlies = []
        for n, i in enumerate(early, len(late)):
            copy = pltpu.make_async_copy(spare[n], refs[len(args) + i], spare[-1].at[n])
            refs[len(args) + i] = Early(copy, spare[n])
            earlies.append(refs[len(args) + i])
        body(*refs)
        for x in lates:
            assert x.copy is None
        for x in earlies:
            x.flush()
        for x in earlies:
            x.copy.wait()

    return pl.pallas_call(
        kernel,
        out_shape=shapes,
        out_specs=[
            pl.BlockSpec(memory_space=pl.ANY if n in hbm_outs or n in early else pltpu.VMEM)
            for n in range(len(outs))
        ],
        in_specs=[pl.BlockSpec(memory_space=m) for m in spaces],
        scratch_shapes=list(scratch) + buffers,
        compiler_params=pltpu.CompilerParams(vmem_limit_bytes=(mib or (56 if late else 16)) * 1024 * 1024),
        cost_estimate=pl.CostEstimate(flops=flops, bytes_accessed=1_000_000, transcendentals=0),
    )(*args)


def fine_forward(
    f, hl, hn, hd, roll, gain, wqkv, wo, bias, lab, send,
    xr_o, xn_o, qkv_o, p_o, c_o, skip_o, b_o, l_o, d_o,
    table,
):
    src = jnp.concatenate([f[...], hl[0:80, :], hn[0:96, :], hd[0:32, :]], 0)
    xr = nn(roll[...], src)
    xr_o[...] = xr.astype(BF)
    xr_o.flush()
    xhat, _ = normalise(xr)
    xn = (xhat * gain[...]).astype(BF)
    xn_o[...] = xn
    xn_o.flush()
    qkv_o[...] = nn(xn, wqkv[...]).astype(BF)
    qkv_o.flush()
    table[...] = jnp.zeros((8, PAD, 128), F32)
    for h in range(8):
        table[h, 0:CELLS, 0:CELLS] = bias[h].astype(F32)
    biases = [table[h, :, 0:PAD].T for h in range(8)]
    for w in range(4):
        allowed = allowed_cells(lab[w : w + 1, :])
        rows = slice(w * PAD, (w + 1) * PAD)
        for h in range(8):
            at = 192 * h
            q = qkv_o[rows, at : at + 64]
            k = qkv_o[rows, at + 64 : at + 128]
            v = qkv_o[rows, at + 128 : at + 192]
            p = probabilities(q, k, biases[h], allowed).astype(BF)
            p_o[w * 8 + h] = p
            c_o[rows, 64 * h : 64 * h + 64] = tn(p, v).astype(BF)
    p_o.flush()
    c_o.flush()
    skip = (xr + nn(c_o[...], wo[...])).astype(BF)
    skip_o[...] = skip
    pieces = nn(send[...], skip).astype(BF)
    b_o[...] = pieces[:64]
    l_o[...] = pieces[64:128]
    d_o[...] = pieces[128:]


def merge_forward(
    win, b, l, d, unroll, order, gain_m, wm, gain_c, send,
    skip_o, pat_o, mn_o, z_o, zn_o, b_o, l_o, d_o,
):
    src = jnp.concatenate([win[...], b[...], l[...], d[...]], 0)
    skip_o[...] = nn(unroll[...], src).astype(BF)
    cells = nn(order[...], src)
    patches = jnp.concatenate([cells[72 * k : 72 * k + 72] for k in range(4)], 1)
    pat_o[...] = patches.astype(BF)
    mhat, _ = normalise(patches)
    mn = (mhat * gain_m[...]).astype(BF)
    mn_o[...] = mn
    z = nn(mn, wm[...]).astype(BF)
    z_o[...] = z
    zhat, _ = normalise(z.astype(F32))
    zn = (zhat * gain_c[...]).astype(BF)
    zn_o[...] = zn
    pieces = nn(send[...], zn).astype(BF)
    b_o[...] = pieces[0:32]
    l_o[...] = pieces[32:64]
    d_o[...] = pieces[64:96]


def first_pieces(f, go, send, lat_o, lon_o, corner_o, tile_o):
    tile = jnp.concatenate([go[r].astype(F32) for r in range(6)], 0).astype(BF)
    tile_o[...] = tile
    pieces = nn(send[...], tile).astype(BF)
    fine = f[...]
    cells = fine.astype(F32).reshape(12, 24, 512)
    lat_o[0:80, :] = fine[0:80]
    lon_o[0:96, :] = cells[:, 0:8].reshape(96, 512).astype(BF)
    corner_o[0:32, :] = cells[0:4, 0:8].reshape(32, 512).astype(BF)
    for i, (o, at) in enumerate(((lat_o, 80), (lon_o, 96), (corner_o, 32))):
        o[at : at + 32, :] = pieces[32 * i : 32 * i + 32, 0:512]
        o[at + 32 : at + 64, :] = pieces[32 * i : 32 * i + 32, 512:]


def pack_weights(w, o, bias, out):
    out[0:192, :] = w[...]
    out[192:256, :] = o[...]
    out[256:272, :] = jnp.zeros((16, 1024), BF)
    for t in range(5):
        n = min(16, CELLS - 16 * t)
        rows = bias[0, 16 * t : 16 * t + n, :]
        out[256 : 256 + n, 128 * t : 128 * t + CELLS] = rows


def coarse_window(tile, b, l, d, own, far, out):
    src = jnp.concatenate([b[...], l[...], d[...]], 0)
    out[...] = (nn(own[...], tile[...]) + nn(far[...], src)).astype(BF)


def coarse_window_labelled(tile, b, l, d, own, far, lab, out):
    parts = []
    for r, at in ((b, 80), (l, 96), (d, 32)):
        parts.append(jnp.concatenate([r[at : at + 32, :], r[at + 32 : at + 64, :]], 1))
    rows = nn(own[...], tile[...]) + nn(far[...], jnp.concatenate(parts, 0))
    at = lax.broadcasted_iota(jnp.int32, rows.shape, 0)
    out[...] = jnp.where(at == CELLS, jnp.broadcast_to(lab[...], rows.shape), rows).astype(BF)


def coarse_attention(
    u0, u1, u2, u3, g0, g1, g2, g3, w0, w1, w2, w3,
    d0, d1, d2, d3, s0, s1, s2, s3, gw0, gw1, gw2, gw3,
    qkv, ctx, dqkv, bias_sum,
):
    ws = (w0, w1, w2, w3)
    u = jnp.concatenate([r[...] for r in (u0, u1, u2, u3)], 0)
    live = lax.broadcasted_iota(jnp.int32, (PAD, 1024), 0) < CELLS
    labels = []
    parts = []
    for r in (g0, g1, g2, g3):
        rows = r[...].astype(F32)
        labels.append(rows[CELLS : CELLS + 1, 0:PAD])
        parts.append(jnp.where(live, rows, 0.0).astype(BF))
    g = jnp.concatenate(parts, 0)
    wo = jnp.concatenate([r[192:256, :] for r in ws], 0)
    dc = nt(g, wo).astype(BF)
    for s in range(4):
        qkv[s] = nt(u, ws[s][0:192, :]).astype(BF)
    masks = [allowed_cells(row) for row in labels]
    for s in range(4):
        groups = [ws[s][256:272, 128 * t : 128 * t + PAD] for t in range(5)]
        bias = jnp.concatenate(groups, 0).astype(F32).T
        total = jnp.zeros((PAD, PAD), F32)
        for w in range(4):
            rows = slice(w * PAD, (w + 1) * PAD)
            q = qkv[s, rows, 0:64]
            k = qkv[s, rows, 64:128]
            v = qkv[s, rows, 128:192]
            p = probabilities(q, k, bias, masks[w])
            pb = p.astype(BF)
            ctx[rows, 64 * s : 64 * s + 64] = tn(pb, v).astype(BF)
            dch = dc[rows, 64 * s : 64 * s + 64]
            ds = score_grad(p, v, dch)
            total = total + ds
            dsb = ds.astype(BF)
            dqkv[s, rows, 0:64] = (tn(dsb, k) * SCALE).astype(BF)
            dqkv[s, rows, 64:128] = (nn(dsb, q) * SCALE).astype(BF)
            dqkv[s, rows, 128:192] = nn(pb, dch).astype(BF)
        bias_sum[s, :, 0:PAD] = total.T
    bias_sum[:, :, PAD:] = jnp.zeros((4, PAD, 128 - PAD), F32)
    c = ctx[...]
    out = nn(c, wo)
    du = nn(dqkv[0], w0[0:192, :])
    for s in range(1, 4):
        du = du + nn(dqkv[s], ws[s][0:192, :])
    for w, (do, so) in enumerate(((d0, s0), (d1, s1), (d2, s2), (d3, s3))):
        do[...] = du[w * PAD : w * PAD + CELLS].astype(BF)
        so[...] = out[w * PAD : w * PAD + CELLS].astype(BF)
    gwo = tn(c, g).astype(BF)
    for s, o in enumerate((gw0, gw1, gw2, gw3)):
        o[0:192, :] = tn(dqkv[s], u).astype(BF)
        o[192:256, :] = gwo[64 * s : 64 * s + 64]
        o[256:272, 640:] = jnp.zeros((16, 384), BF)
        for t in range(5):
            o[256:272, 128 * t : 128 * t + 128] = bias_sum[s, 16 * t : 16 * t + 16].astype(BF)


def coarse_sum(a0, a1, a2, a3, back, own_o, b_o, l_o, d_o):
    total = a0[...].astype(F32) + a1[...].astype(F32) + a2[...].astype(F32) + a3[...].astype(F32)
    total = total.astype(BF)
    own_o[...] = total
    pieces = nn(back[...], total).astype(BF)
    b_o[...] = pieces[0:32]
    l_o[...] = pieces[32:64]
    d_o[...] = pieces[64:96]


def coarse_output(z, own, b, l, d, uown, ufar, out_o):
    far = jnp.concatenate([b[...], l[...], d[...]], 0)
    s = nn(uown[...], own[...]) + nn(ufar[...], far)
    rows = z[...].astype(F32) + s
    for r in range(6):
        out_o[r] = rows[12 * r : 12 * r + 12].astype(BF)


def merge_backward(
    at, z, go, own, b, l, d, uown, ufar, gain_c, pat, gain_m, wm, gskip, spread,
    dskip_o, top_o, side_o, corner_o, gg_m, gg_c, *dz_os,
):
    far = jnp.concatenate([b[...], l[...], d[...]], 0)
    dzn = nn(uown[...], own[...]) + nn(ufar[...], far)
    z32 = z[...].astype(F32)
    zhat, rstd = normalise(z32)
    gg_c[...] = jnp.sum(dzn * zhat, 0, keepdims=True)
    dz = (go[...].astype(F32) + norm_back(dzn, gain_c[...], zhat, rstd)).astype(BF)
    table = dz_os[4]
    table[...] = dz
    for k in range(4):
        dz_os[k][...] = table[:, pl.ds(pl.multiple_of((at[0] + k) % 4 * 256, 256), 256)]
    dmn = nt(dz, wm[...])
    mhat, mrstd = normalise(pat[...].astype(F32))
    gg_m[...] = jnp.sum(dmn * mhat, 0, keepdims=True)
    dpat = norm_back(dmn, gain_m[...], mhat, mrstd).astype(BF)
    cells = jnp.concatenate([dpat[:, 512 * k : 512 * k + 512] for k in range(4)], 0)
    dskip = (gskip[...].astype(F32) + nn(spread[...], cells)).astype(BF)
    dskip_o[...] = dskip
    top_o[...] = dskip[0:80]
    cells = dskip.astype(F32).reshape(12, 24, 512)
    side_o[...] = cells[:, 0:8].reshape(96, 512).astype(BF)
    corner_o[...] = cells[0:4, 0:8].reshape(32, 512).astype(BF)


def fine_backward(
    core, f, hl, hn, hd, roll, gain, wqkv, wo, xr, xn, qkv, p_in, c, send, gg_m, gg_c,
    dx_o, b_o, l_o, d_o, keep_o, give_o,
    dqkv, bias_sum, pack_o, sems,
):
    src = jnp.concatenate([f[...], hl[...], hn[...], hd[...]], 0)
    g32 = nn(roll[...], src)
    g = g32.astype(BF)
    dc = nt(g, wo[...]).astype(BF)
    bias_sum[...] = jnp.zeros((8, PAD, 128), F32)
    for h in range(8):
        at = 192 * h
        total = jnp.zeros((PAD, PAD), F32)
        for w in range(4):
            rows = slice(w * PAD, (w + 1) * PAD)
            q = qkv[rows, at : at + 64]
            k = qkv[rows, at + 64 : at + 128]
            v = qkv[rows, at + 128 : at + 192]
            pb = p_in[w * 8 + h]
            dch = dc[rows, 64 * h : 64 * h + 64]
            ds = score_grad(pb.astype(F32), v, dch)
            total = total + ds
            dsb = ds.astype(BF)
            dqkv[rows, at : at + 64] = (tn(dsb, k) * SCALE).astype(BF)
            dqkv[rows, at + 64 : at + 128] = (nn(dsb, q) * SCALE).astype(BF)
            dqkv[rows, at + 128 : at + 192] = nn(pb, dch).astype(BF)
        bias_sum[h, :, 0:PAD] = total
    dproj = dqkv[...]
    du = nt(dproj, wqkv[...])
    xhat, rstd = normalise(xr[...].astype(F32))
    gg_f = jnp.sum(du * xhat, 0, keepdims=True)
    dx = (g32 + norm_back(du, gain[...], xhat, rstd)).astype(BF)
    dx_o[...] = dx
    pieces = nn(send[...], dx).astype(BF)
    b_o[...] = pieces[:64]
    l_o[...] = pieces[64:128]
    d_o[...] = pieces[128:]
    gq = tn(xn[...], dproj)
    for i in range(12):
        pack_o[32 * i : 32 * i + 32] = gq[:, 128 * i : 128 * i + 128].reshape(32, 16, 128).astype(BF)
    go = tn(c[...], g)
    for i in range(4):
        pack_o[384 + 32 * i : 416 + 32 * i] = (
            go[:, 128 * i : 128 * i + 128].reshape(32, 16, 128).astype(BF)
        )
    for h in range(8):
        pack_o[512 + 5 * h : 517 + 5 * h] = bias_sum[h].reshape(5, 16, 128).astype(BF)
    rows = [gg_f[:, 128 * i : 128 * i + 128] for i in range(4)]
    rows += [gg_m[:, 128 * i : 128 * i + 128] for i in range(16)]
    rows += [gg_c[:, 128 * i : 128 * i + 128] for i in range(8)]
    rows.append(jnp.zeros((4, 128), F32))
    pack_o[552:554] = jnp.concatenate(rows, 0).reshape(2, 16, 128).astype(BF)
    pack_o[554:PARTS] = jnp.zeros((PARTS - 554, 16, 128), BF)

    copies = [
        pltpu.make_async_copy(pack_o.at[pl.ds(start, HALF)], o, sems.at[n])
        for n, (o, start) in enumerate(
            ((keep_o, core[0] * HALF), (give_o, (1 - core[0]) * HALF))
        )
    ]
    for x in copies:
        x.start()
    for x in copies:
        x.wait()


def merge_weight_share(core, *refs):
    total = tn(refs[0][...], refs[4][...])
    for k in range(1, 4):
        total = total + tn(refs[k][...], refs[4 + k][...])
    keep_o, give_o = refs[8], refs[9]

    def halves(first, second):
        first[0:64, :] = total[0:64].astype(BF)
        second[0:64, :] = total[64:128].astype(BF)
        first[64:128, :] = total[128:192].astype(BF)
        second[64:128, :] = total[192:256].astype(BF)

    @pl.when(core[0] == 0)
    def _():
        halves(keep_o, give_o)

    @pl.when(core[0] != 0)
    def _():
        halves(give_o, keep_o)


def pack_sums(at, g0, r0, g2, r2, keep, got, out):
    for a, (g, r) in ((at[0], (g0, r0)), (1 - at[0], (g2, r2))):
        head = (g[...].astype(F32) + r[...].astype(F32)).astype(BF)
        for j in range(8):
            row = pl.multiple_of(a * 3200 + 400 * j, 16)
            out[pl.ds(row, 272), :] = head[:, 128 * j : 128 * j + 128]
    merge = keep[...].astype(F32) + got[...].astype(F32)
    for q in range(16):
        rows = merge[8 * q : 8 * q + 8]
        for t in range(8):
            pair = [rows[:, 256 * t : 256 * t + 128], rows[:, 256 * t + 128 : 256 * t + 256]]
            row = 400 * q + 272 + 16 * t
            out[row : row + 16, :] = jnp.concatenate(pair, 0).astype(BF)


def unpack_sums(parts, strip_o, merge_o):
    total = parts[0:400, :].astype(F32)
    for q in range(1, 16):
        total = total + parts[400 * q : 400 * q + 400, :].astype(F32)
    strip_o[...] = total[0:272].astype(BF)
    for t in range(16):
        merge_o[:, 128 * t : 128 * t + 128] = total[272 + 8 * t : 280 + 8 * t]


def coarse_join(at, *refs):
    parts, (gw_o, go_o, gb_o, table) = refs[:4], refs[4:]
    for k in range(4):
        for n in range(2):
            lon = (at[0] + k) % 4 * 2 + (at[1] + n) % 2
            lanes = pl.ds(pl.multiple_of(lon * 128, 128), 128)
            rows = parts[k][272 * n : 272 * n + 272, :].astype(F32)
            gw_o[:, lanes] = rows[0:192]
            go_o[:, lanes] = rows[192:256]
            table[:, lanes] = rows[256:272]
    for t in range(5):
        n = min(16, CELLS - 16 * t)
        gb_o[0, 16 * t : 16 * t + n, :] = table[0:n, 128 * t : 128 * t + CELLS]


def fine_place(win, b, l, d, unroll, out):
    src = jnp.concatenate([win[...], b[...], l[...], d[...]], 0)
    out[...] = nn(unroll[...], src).astype(BF)


def add_two(a, b, out):
    out[...] = (a[...].astype(F32) + b[...].astype(F32)).astype(BF)


def sum_and_copy(parts, out):
    total = parts[0].astype(F32)
    for k in range(1, 64):
        total = total + parts[k].astype(F32)
    total = total.astype(BF)
    for k in range(64):
        out[k] = total


def unpack(core, mine, other, gq_o, gb_o, go_o, gf_o, gm_o, gc_o, pack):
    @pl.when(core[0] == 0)
    def _():
        pack[0:HALF] = mine[...]
        pack[HALF:PARTS] = other[...]

    @pl.when(core[0] != 0)
    def _():
        pack[0:HALF] = other[...]
        pack[HALF:PARTS] = mine[...]

    for i in range(12):
        gq_o[:, 128 * i : 128 * i + 128] = (
            pack[32 * i : 32 * i + 32].astype(F32).reshape(512, 128)
        )
    for i in range(4):
        go_o[:, 128 * i : 128 * i + 128] = (
            pack[384 + 32 * i : 416 + 32 * i].astype(F32).reshape(512, 128)
        )
    for h in range(8):
        t = pack[512 + 5 * h : 517 + 5 * h].astype(F32).reshape(80, 128)
        gb_o[h] = t[:, 0:PAD].T[0:CELLS, 0:CELLS]
    rows = pack[552:554].astype(F32).reshape(32, 128)
    first = 0
    for o, n in ((gf_o, 4), (gm_o, 16), (gc_o, 8)):
        for i in range(n):
            o[:, 128 * i : 128 * i + 128] = rows[first + i : first + i + 1]
        first += n


def count_of(axes):
    n = 1
    for a in axes:
        n *= lax.axis_size(a)
    return n


def shift(x, axes, by):
    n = count_of(axes)
    return lax.ppermute(x, axes, [(i, (i + by) % n) for i in range(n)])


def shift_both(x, by):
    nl, nn_ = count_of(LAT), count_of(LON)
    pairs = [
        (i * nn_ + j, ((i + by) % nl) * nn_ + (j + by) % nn_)
        for i in range(nl)
        for j in range(nn_)
    ]
    return lax.ppermute(x, ALL, pairs)


def exchange(pieces, by):
    lat_piece, lon_piece, corner = pieces
    return shift(lat_piece, LAT, by), shift(lon_piece, LON, by), shift_both(corner, by)


def along_y(x):
    return [x] + [shift(x, ("y",), -k) for k in (1, 2, 3)]


def back_along_y(parts):
    return [parts[0]] + [shift(parts[k], ("y",), k) for k in (1, 2, 3)]


def after(x, *others):
    return lax.optimization_barrier((x, others))[0]


def local(
    fields,
    region_fine,
    region_coarse,
    gain_fine,
    qkv_fine,
    bias_fine,
    out_fine,
    gain_merge,
    merge_weight,
    gain_coarse,
    qkv_coarse,
    bias_coarse,
    out_coarse,
    grad_skip,
    grad_out,
):
    c_roll, c_send, c_unroll = make_fine_roll(), make_fine_send(), make_fine_unroll()
    roll_own, roll_far = make_coarse_roll()
    back_own, back_far = make_coarse_unroll()
    roll_f, send_f, unroll_f = const(c_roll), const(c_send), const(c_unroll)
    order_f = const(c_unroll[patch_order()])
    spread = np.zeros((288, 288), np.float32)
    spread[patch_order(), np.arange(288)] = 1
    spread_f = const(spread)
    send_c, back_c = const(make_coarse_send()), const(make_coarse_back())
    roll_own, roll_far = const(roll_own), const(roll_far)
    back_own, back_far = const(back_own), const(back_far)
    gain_f2, gain_m2, gain_c2 = gain_fine[None], gain_merge[None], gain_coarse[None]

    core = lax.axis_index("c").astype(jnp.int32).reshape(1)
    tile = fields.reshape(288, 512)
    piece = ((32, 1024), BF)
    win = ((320, 512), BF)
    window = ((PAD, 1024), BF)

    *first, go_tile = call(
        first_pieces,
        [((144, 512), BF), ((160, 512), BF), ((96, 512), BF), ((72, 1024), BF)],
        tile, grad_out, send_c,
        late="all",
    )
    first_far = exchange(first, -1)

    (w0,) = call(pack_weights, [((272, 1024), BF)], qkv_coarse.T, out_coarse, bias_coarse)
    w2 = shift(w0, ("xh",), 1)
    w1 = shift(w0, ("c",), 1)

    label_c = jnp.pad(
        region_coarse.reshape(1, 72).astype(F32), ((0, 0), (0, 952)), constant_values=-1.0
    )
    label_f = region_fine.reshape(2, 6, 2, 12).transpose(0, 2, 1, 3).reshape(4, 72).astype(F32)
    label_f = jnp.pad(label_f, ((0, 0), (0, 8)), constant_values=-1.0)

    (gw_win,) = call(
        coarse_window_labelled, [window], go_tile, *first_far, roll_own, roll_far, label_c
    )
    g_all = along_y(gw_win)
    xr, xn, qkv, prob, ctx, skip_win, *skip_pieces = call(
        fine_forward,
        [win, win, ((320, 1536), BF), ((32, PAD, PAD), BF), win, win,
         ((64, 512), BF), ((64, 512), BF), ((32, 512), BF)],
        after(tile, gw_win), *first_far, roll_f, gain_f2, qkv_fine, out_fine, bias_fine, label_f, send_f,
        late="all",
        scratch=[pltpu.VMEM((8, PAD, 128), F32)],
        early=(0, 1, 2, 3, 4),
        flops=3_000_000_000,
    )
    s_far = exchange(skip_pieces, 1)
    skip_win = after(skip_win, g_all)
    skip_level, pat, mn, z, zn, *z_pieces = call(
        merge_forward,
        [((288, 512), BF), ((72, 2048), BF), ((72, 2048), BF), ((72, 1024), BF), ((72, 1024), BF),
         piece, piece, piece],
        skip_win, *s_far, unroll_f, order_f, gain_m2, merge_weight, gain_c2, send_c,
        late="all",
        flops=2_500_000_000,
    )
    z_far = exchange(z_pieces, -1)
    (u_win,) = call(coarse_window, [window], zn, *z_far, roll_own, roll_far)
    w3 = shift(after(w2, u_win), ("c",), 1)
    u_all = along_y(u_win)
    outs = call(
        coarse_attention,
        [((CELLS, 1024), BF)] * 8 + [((272, 1024), BF)] * 4,
        *u_all, *g_all, w0, w1, w2, w3,
        late="all",
        scratch=[
            pltpu.VMEM((4, 320, 192), BF), pltpu.VMEM((320, 256), BF),
            pltpu.VMEM((4, 320, 192), BF), pltpu.VMEM((4, PAD, 128), F32),
        ],
        flops=9_000_000_000,
    )
    gw0, gw1, gw2, gw3 = outs[8:]
    du_parts = back_along_y(outs[0:4])
    r0 = shift(gw1, ("c",), 1)
    r2 = shift(gw3, ("c",), 1)
    du_parts[0] = after(du_parts[0], r0, r2)
    du_win, *du_pieces = call(coarse_sum, [((CELLS, 1024), BF)] + [piece] * 3, *du_parts, back_c)
    du_far = exchange(du_pieces, 1)
    mn_own = after(mn, du_win)
    mn_all = [mn_own] + [shift(mn_own, ("y",), k) for k in (1, 2, 3)]
    at_y = lax.axis_index("y").astype(jnp.int32).reshape(1)
    dskip, k_lat, k_lon, k_corner, gg_m, gg_c, *dz_parts = call(
        merge_backward,
        [((288, 512), BF), ((80, 512), BF), ((96, 512), BF), ((32, 512), BF),
         ((1, 2048), F32), ((1, 1024), F32)] + [((72, 256), BF)] * 4,
        at_y, z, go_tile, du_win, *du_far, back_own, back_far, gain_c2, pat, gain_m2, merge_weight,
        grad_skip.reshape(288, 512), spread_f,
        scratch=[pltpu.VMEM((72, 1024), BF)],
        scalars=1,
        late="all",
        flops=3_000_000_000,
    )
    k_far = exchange((k_lat, k_lon, k_corner), -1)
    dz_all = dz_parts[0:1] + [shift(dz_parts[k], ("y",), k) for k in (1, 2, 3)]
    merge_keep, merge_give = call(
        merge_weight_share, [((128, 2048), BF)] * 2, core, *dz_all, *mn_all, scalars=1, late="all"
    )
    merge_got = shift(merge_give, ("c",), 1)
    xh = lax.axis_index("xh").astype(jnp.int32).reshape(1)
    (packed,) = call(
        pack_sums, [((6400, 128), BF)], xh, gw0, r0, gw2, r2, merge_keep, merge_got, scalars=1
    )
    packed = after(packed, k_far)
    sums = lax.all_to_all(packed, ("xh",) + LON, 0, 0, tiled=True)
    dskip = after(dskip, packed)
    dx_win, d_lat, d_lon, d_corner, keep, give = call(
        fine_backward,
        [win, ((64, 512), BF), ((64, 512), BF), ((32, 512), BF),
         ((HALF, 16, 128), BF), ((HALF, 16, 128), BF)],
        core, dskip, *k_far, roll_f, gain_f2, qkv_fine, out_fine, xr, xn, qkv, prob, ctx, send_f,
        gg_m, gg_c,
        late="all",
        scratch=[
            pltpu.VMEM((320, 1536), BF), pltpu.VMEM((8, PAD, 128), F32),
            pltpu.VMEM((PARTS, 16, 128), BF), pltpu.SemaphoreType.DMA((2,)),
        ],
        scalars=1,
        hbm_outs=(4, 5),
        flops=1_000_000,
    )


    strip, merge_t = call(unpack_sums, [((272, 128), BF), ((8, 2048), F32)], sums)
    at_lon = jnp.stack([lax.axis_index("z"), lax.axis_index("xl")]).astype(jnp.int32)

    s_parts = back_along_y([after(x, dx_win) for x in outs[4:8]])
    keep = after(keep, sums, s_parts)
    s_win, s_lat, s_lon, s_corner = call(coarse_sum, [((CELLS, 1024), BF)] + [piece] * 3, *s_parts, back_c)
    (half,) = call(add_two, [((HALF, 16, 128), BF)], keep, shift(give, ("c",), 1), late="all")
    half = after(half, s_corner, strip)
    by_chip = (count_of(CHIPS), HALF * 16 // count_of(CHIPS), 128)
    spread_out = lax.all_to_all(half.reshape(by_chip), CHIPS, 0, 0, tiled=True)
    d_far = exchange((d_lat, d_lon, d_corner), 1)
    s_corner = shift_both(s_corner, 1)
    strips = jnp.concatenate([strip, shift(strip, ("xl",), 1)], 0)
    (copies,) = call(sum_and_copy, [(by_chip, BF)], spread_out)
    copies = after(copies, d_far, s_corner, strips)
    whole_half = lax.all_to_all(copies, CHIPS, 0, 0, tiled=True).reshape(HALF, 16, 128)
    strips, s_lat, s_lon = after((strips, s_lat, s_lon), copies)
    strips = [strips] + [shift(strips, ("z",), -k) for k in (1, 2, 3)]
    s_back = (shift(s_lat, LAT, 1), shift(s_lon, LON, 1), s_corner)
    (output,) = call(
        coarse_output, [((6, 12, 1024), BF)], z, s_win, *s_back, back_own, back_far
    )
    (grad_fields,) = call(fine_place, [((288, 512), BF)], dx_win, *d_far, unroll_f)
    gw_c, go_c, gb_c = call(
        coarse_join, [((192, 1024), F32), ((64, 1024), F32), ((1, CELLS, CELLS), F32)],
        at_lon, *strips,
        scratch=[pltpu.VMEM((16, 1024), F32)], scalars=1,
    )
    whole_half = after(whole_half, merge_t, gw_c, output, grad_fields)
    other_half = shift(whole_half, ("c",), 1)

    gq, gb, go, gg_f, gg_m, gg_c = call(
        unpack,
        [((512, 1536), F32), ((8, CELLS, CELLS), F32), ((512, 512), F32),
         ((1, 512), F32), ((1, 2048), F32), ((1, 1024), F32)],
        core, whole_half, other_half,
        scratch=[pltpu.VMEM((PARTS, 16, 128), BF)],
        scalars=1,
    )
    return (
        skip_level.reshape(12, 24, 512),
        output,
        grad_fields.reshape(12, 24, 512),
        gg_f[0],
        gq,
        gb,
        go,
        gg_m[0],
        merge_t.T,
        gg_c[0],
        gw_c.T,
        gb_c,
        go_c,
    )


def solution(mesh):
    fine_mesh = Mesh(mesh.devices.reshape(4, 2, 2, 4, 2), ALL)
    grid = P(LAT, LON, None)
    placed = (
        grid,
        P(LAT, LON),
        P(LAT, LON),
        P(),
        P(),
        P(),
        P(),
        P(),
        P(),
        P(),
        P(None, LAT),
        P(LAT, None, None),
        P(LAT, None),
        grid,
        grid,
    )
    return jax.shard_map(
        local,
        mesh=fine_mesh,
        in_specs=placed,
        out_specs=(
            grid,
            grid,
            grid,
            P(),
            P(),
            P(),
            P(),
            P(),
            P(None, ALL),
            P(),
            P(None, LAT),
            P(LAT, None, None),
            P(LAT, None),
        ),
        check_vma=False,
    )
```
